128 devices in a mesh: seq: 128 (over y, x, z, core).
Axes of the slice: x: 4, y: 4, z: 4, core: 2. Of those that a mesh axis runs over, the one named last changes fastest.
Arguments:
- tokens: bfloat16 [32768, 640], P('seq'), may hold values from -6 to 6
- starts: int32 [128], replicated, may hold values from 0 to 1, as said below
- query_weight: bfloat16 [640, 1024], P('seq'), may hold values from -0.25 to 0.25
- key_weight: bfloat16 [640, 256], P('seq'), may hold values from -0.25 to 0.25
- value_weight: bfloat16 [640, 256], P('seq'), may hold values from -0.25 to 0.25
- output_weight: bfloat16 [1024, 640], P('seq'), may hold values from -0.1875 to 0.1875
- gate_weight: bfloat16 [640, 2048], P('seq'), may hold values from -0.25 to 0.25
- up_weight: bfloat16 [640, 2048], P('seq'), may hold values from -0.25 to 0.25
- down_weight: bfloat16 [2048, 640], P('seq'), may hold values from -0.125 to 0.125
- input_gain: float32 [640], replicated, may hold values from 0.25 to 1.75
- query_gain: float32 [256], replicated, may hold values from 0.25 to 1.75
- key_gain: float32 [256], replicated, may hold values from 0.25 to 1.75
- attn_gain: float32 [640], replicated, may hold values from 0.25 to 1.75
- ffn_gain: float32 [640], replicated, may hold values from 0.25 to 1.75
- ffn_out_gain: float32 [640], replicated, may hold values from 0.25 to 1.75
- cotangent: bfloat16 [32768, 640], P('seq'), may hold values from -6 to 6
Outputs:
- output: bfloat16 [32768, 640], P('seq')
- input_grad: bfloat16 [32768, 640], P('seq')
- grad_query_weight: float32 [640, 1024], P('seq')
- grad_key_weight: float32 [640, 256], P('seq')
- grad_value_weight: float32 [640, 256], P('seq')
- grad_output_weight: float32 [1024, 640], P('seq')
- grad_gate_weight: float32 [640, 2048], P('seq')
- grad_up_weight: float32 [640, 2048], P('seq')
- grad_down_weight: float32 [2048, 640], P('seq')
- grad_input_gain: float32 [640], replicated
- grad_query_gain: float32 [256], replicated
- grad_key_gain: float32 [256], replicated
- grad_attn_gain: float32 [640], replicated
- grad_ffn_gain: float32 [640], replicated
- grad_ffn_out_gain: float32 [640], replicated
The draws below stay inside these ranges and needn't reach their ends.
Inputs may be any that keep to these rules, and one draw needn't show every extreme that they name: starts[0] is 1; a sequence runs from a group with starts 1 up to the next such group; every sequence but the last holds between max(1, 8) and max(1, 32) groups, the last ends with the array.
All inputs are finite; a program needn't handle non-finite values.
Results may differ from the reference program's by a relative error of at most 0.019.
Values may be sent and summed in bfloat16 or wider, within the bound.
No kernel may reach another device: no remote copies, remote signals or barrier semaphores. Data moves between devices by JAX's collectives and lax.ppermute only.
A program may use at most 128 MiB of HBM per device.

```python
import math
import jax
import jax.numpy as jnp
from jax import lax

D = 640
FF = 2048
HEADS = 4
HEAD_DIM = 256
WINDOW = 512
TOK_DEV = 256
SEQ_MIN = 2048
SEQ_MAX = 8192
HQ = 1024
GROUPS = 128
TOKENS = 32768


def draw_starts(key, part):
    key = jax.random.fold_in(key, 7)
    shortest = max(1, SEQ_MIN // TOK_DEV)
    longest = max(shortest, SEQ_MAX // TOK_DEV)
    spans = jax.random.randint(key, (GROUPS,), shortest, longest + 1).astype(jnp.int32)
    begins = jnp.concatenate([jnp.zeros((1,), jnp.int32), jnp.cumsum(spans)[:-1].astype(jnp.int32)])
    return jnp.zeros((GROUPS,), jnp.int32).at[begins].set(1, mode='drop')


def shard_levels(key, shape, pieces, smallest, largest):
    level, own = 1.0, jax.random.fold_in(key, 6)
    for dim, blocks in pieces:
        draws = jnp.exp(jax.random.uniform(jax.random.fold_in(own, dim), (blocks,), jnp.float32, smallest / len(pieces), largest / len(pieces)))
        level = level * jnp.repeat(draws, shape[dim] // blocks).reshape([-1 if axis == dim else 1 for axis in range(len(shape))])
    return level


def normal_values(rng, extent, spread, limit, shards=(), kind=jnp.bfloat16):
    factor_of = shard_levels(rng, extent, shards, -0.22, 0.18) if shards else 1.0
    values = jax.random.normal(rng, extent, jnp.float32) * spread * factor_of
    return jnp.minimum(jnp.maximum(values, -limit), limit).astype(kind)


def setup_inputs(seed: int = 0) -> dict:
    splits = jax.random.split(jax.random.key(seed), 17)
    return {
        "tokens": normal_values(splits[0], (TOKENS, D), 1.0, 6.0, ((0, 128),)),
        "starts": draw_starts(jax.random.fold_in(splits[16], 71), 0),
        "query_weight": normal_values(splits[2], (D, HQ), D ** -0.5, 0.25, ((0, 128),)),
        "key_weight": normal_values(splits[3], (D, HEAD_DIM), D ** -0.5, 0.25, ((0, 128),)),
        "value_weight": normal_values(splits[4], (D, HEAD_DIM), D ** -0.5, 0.25, ((0, 128),)),
        "output_weight": normal_values(splits[5], (HQ, D), HQ ** -0.5, 0.1875, ((0, 128),)),
        "gate_weight": normal_values(splits[6], (D, FF), D ** -0.5, 0.25, ((0, 128),)),
        "up_weight": normal_values(splits[7], (D, FF), D ** -0.5, 0.25, ((0, 128),)),
        "down_weight": normal_values(splits[8], (FF, D), FF ** -0.5, 0.125, ((0, 128),)),
        "input_gain": jnp.clip(1.0 + 0.15 * jax.random.normal(splits[9], (D,), jnp.float32), 0.25, 1.75),
        "query_gain": jnp.clip(1.0 + 0.15 * jax.random.normal(splits[10], (HEAD_DIM,), jnp.float32), 0.25, 1.75),
        "key_gain": jnp.clip(1.0 + 0.15 * jax.random.normal(splits[11], (HEAD_DIM,), jnp.float32), 0.25, 1.75),
        "attn_gain": jnp.clip(1.0 + 0.15 * jax.random.normal(splits[12], (D,), jnp.float32), 0.25, 1.75),
        "ffn_gain": jnp.clip(1.0 + 0.15 * jax.random.normal(splits[13], (D,), jnp.float32), 0.25, 1.75),
        "ffn_out_gain": jnp.clip(1.0 + 0.15 * jax.random.normal(splits[14], (D,), jnp.float32), 0.25, 1.75),
        "cotangent": normal_values(splits[15], (TOKENS, D), 1.0, 6.0, ((0, 128),)),
    }


norm_epsilon = 1e-06
rope_base = 10000.0
highest = lax.Precision.HIGHEST

@jax.custom_vjp
def low(v):
    return lax.optimization_barrier(v.astype(jnp.bfloat16)).astype(jnp.float32)

@jax.custom_vjp
def low_back(v):
    return v

def low_keep(v):
    return (low(v), None)

def low_pass(kept, grad):
    return (grad,)

def back_keep(v):
    return (v, None)

def back_low(kept, grad):
    return (low(grad),)
low.defvjp(low_keep, low_pass)
low_back.defvjp(back_keep, back_low)

def rms_scale(values, gain):
    mean_square = lax.optimization_barrier(jnp.mean(values * values, axis=-1, keepdims=True))
    return values * lax.rsqrt(mean_square + norm_epsilon) * gain

def rope_tables(position, head_dim):
    half = head_dim // 2
    exponent = jnp.arange(half, dtype=jnp.float32) * (2.0 / head_dim)
    inverse = jnp.power(jnp.float32(rope_base), -exponent)
    angles = position.astype(jnp.float32)[:, None] * inverse[None, :]
    return (jnp.cos(angles)[:, None, :], jnp.sin(angles)[:, None, :])

def head_prep(pre, gain, cosine, sine):
    normed = rms_scale(pre, gain)
    half = normed.shape[-1] // 2
    first = normed[..., :half]
    second = normed[..., half:]
    return jnp.concatenate([first * cosine - second * sine, second * cosine + first * sine], axis=-1)

def matmul(left, right):
    return jnp.dot(left, right, precision=highest)

def attention(queries, keys, values, seq_first):
    block = min(512, TOKENS)
    count = TOKENS // block
    width = block + WINDOW
    scale = 1.0 / math.sqrt(HEAD_DIM)
    pad_keys = jnp.concatenate([jnp.zeros((WINDOW, HEAD_DIM), jnp.float32), keys], axis=0)
    pad_values = jnp.concatenate([jnp.zeros((WINDOW, HEAD_DIM), jnp.float32), values], axis=0)
    index = (jnp.arange(count, dtype=jnp.int32)[:, None] * block + jnp.arange(width, dtype=jnp.int32)[None, :]).astype(jnp.int32)
    key_blocks = pad_keys[index]
    value_blocks = pad_values[index]
    query_blocks = queries.reshape(count, block, HEADS, HEAD_DIM)
    first_blocks = seq_first.reshape(count, block)
    bases = (jnp.arange(count, dtype=jnp.int32) * block).astype(jnp.int32)

    def one_block(inputs):
        query_block, key_block, value_block, first_block, base = inputs
        query_index = base + jnp.arange(block, dtype=jnp.int32)
        key_index = base - WINDOW + jnp.arange(width, dtype=jnp.int32)
        gap = query_index[:, None] - key_index[None, :]
        valid = (gap >= 0) & (gap < WINDOW) & (key_index[None, :] >= first_block[:, None])
        scores = jnp.einsum('qhd,kd->hqk', query_block, key_block, precision=highest) * scale
        scores = low_back(scores)
        scores = jnp.where(valid[None, :, :], scores, -1e+30)
        peak = lax.optimization_barrier(jnp.max(scores, axis=-1, keepdims=True))
        weights = jnp.exp(scores - peak)
        probs = weights / lax.optimization_barrier(jnp.sum(weights, axis=-1, keepdims=True))
        probs = low(probs)
        return jnp.einsum('hqk,kd->qhd', probs, value_block, precision=highest)
    result = lax.map(jax.checkpoint(one_block), (query_blocks, key_blocks, value_blocks, first_blocks, bases))
    return result.reshape(TOKENS, HQ)

def forward(tokens, query_weight, key_weight, value_weight, output_weight, gate_weight, up_weight, down_weight, input_gain, query_gain, key_gain, attn_gain, ffn_gain, ffn_out_gain, position, seq_first):
    normed_in = low(rms_scale(tokens, input_gain))
    query_pre = low_back(matmul(normed_in, query_weight)).reshape(TOKENS, HEADS, HEAD_DIM)
    key_pre = low_back(matmul(normed_in, key_weight)).reshape(TOKENS, 1, HEAD_DIM)
    values = low(low_back(matmul(normed_in, value_weight)))
    cosine, sine = rope_tables(position, HEAD_DIM)
    queries = low(low_back(head_prep(query_pre, query_gain, cosine, sine)))
    keys = low(low_back(head_prep(key_pre, key_gain, cosine, sine)))[:, 0, :]
    attended = low(low_back(attention(queries, keys, values, seq_first)))
    projected = low_back(matmul(attended, output_weight))
    resid = tokens + rms_scale(projected, attn_gain)
    rows = min(4096, TOKENS)

    def ffn_block(resid_block):
        normed_ffn = low(rms_scale(resid_block, ffn_gain))
        gate = low_back(matmul(normed_ffn, gate_weight))
        upward = low_back(matmul(normed_ffn, up_weight))
        mixed = low(jax.nn.gelu(gate, approximate=True) * upward)
        down = low_back(matmul(mixed, down_weight))
        return rms_scale(down, ffn_out_gain)
    branch = lax.map(jax.checkpoint(ffn_block), resid.reshape(TOKENS // rows, rows, D))
    return resid + branch.reshape(TOKENS, D)

def reference(tokens, starts, query_weight, key_weight, value_weight, output_weight, gate_weight, up_weight, down_weight, input_gain, query_gain, key_gain, attn_gain, ffn_gain, ffn_out_gain, cotangent):
    group_ids = jnp.arange(GROUPS, dtype=jnp.int32)
    first_group = lax.cummax(jnp.where(starts == 1, group_ids, 0).astype(jnp.int32), axis=0)
    token_ids = jnp.arange(TOKENS, dtype=jnp.int32)
    seq_first = (first_group[token_ids // TOK_DEV] * TOK_DEV).astype(jnp.int32)
    position = (token_ids - seq_first).astype(jnp.int32)
    inputs = (tokens.astype(jnp.float32), query_weight.astype(jnp.float32), key_weight.astype(jnp.float32), value_weight.astype(jnp.float32), output_weight.astype(jnp.float32), gate_weight.astype(jnp.float32), up_weight.astype(jnp.float32), down_weight.astype(jnp.float32), input_gain.astype(jnp.float32), query_gain.astype(jnp.float32), key_gain.astype(jnp.float32), attn_gain.astype(jnp.float32), ffn_gain.astype(jnp.float32), ffn_out_gain.astype(jnp.float32))

    def layer(*floats):
        return forward(*floats, position, seq_first)
    result, pullback = jax.vjp(layer, *inputs)
    grads = pullback(cotangent.astype(jnp.float32))
    return (result.astype(jnp.bfloat16), grads[0].astype(jnp.bfloat16), grads[1], grads[2], grads[3], grads[4], grads[5], grads[6], grads[7], grads[8], grads[9], grads[10], grads[11], grads[12], grads[13])
```

```python
from functools import partial
import math

import jax
import jax.numpy as jnp
from jax import lax
from jax.sharding import Mesh, PartitionSpec as P

WINDOW = 512
ALL = ("y", "x", "z", "c")

norm_epsilon = 1e-06
rope_base = 10000.0
bf16 = jnp.bfloat16
f32 = jnp.float32


def shifted(value, steps):
    count = lax.axis_size(ALL)
    leading, last = (max(0, -steps), min(count, count - steps))
    return lax.ppermute(value, ALL, [(source, source + steps) for source in range(leading, last)])


def rms_scale(values, gain):
    mean_square = jnp.mean(values * values, axis=-1, keepdims=True)
    return values * lax.rsqrt(mean_square + norm_epsilon) * gain


def rope_tables(position, head_dim):
    half = head_dim // 2
    exponent = jnp.arange(half, dtype=jnp.float32) * (2.0 / head_dim)
    inverse = jnp.power(jnp.float32(rope_base), -exponent)
    angles = position.astype(jnp.float32)[:, None] * inverse[None, :]
    return (jnp.cos(angles)[:, None, :], jnp.sin(angles)[:, None, :])


def head_prep(pre, gain, cosine, sine):
    normed = rms_scale(pre, gain)
    half = normed.shape[-1] // 2
    first = normed[..., :half]
    second = normed[..., half:]
    return jnp.concatenate(
        [first * cosine - second * sine, second * cosine + first * sine], axis=-1
    )


def gated(gate, upward):
    return jax.nn.gelu(gate, approximate=True) * upward


def product(left, right):
    return jnp.dot(left, right, preferred_element_type=jnp.float32)


def transposed_left(left, right):
    return lax.dot_general(
        left, right, (((0,), (0,)), ((), ())), preferred_element_type=jnp.float32
    )


def transposed_right(left, right):
    return lax.dot_general(
        left, right, (((1,), (1,)), ((), ())), preferred_element_type=jnp.float32
    )


def swap_core(value):
    return lax.ppermute(value, "c", [(0, 1), (1, 0)])


def split_columns(grads):
    core = lax.axis_index("c")
    mine, theirs = [], []
    for grad in grads:
        half = grad.shape[1] // 2
        first, second = grad[:, :half], grad[:, half:]
        mine.append(jnp.where(core == 0, first, second))
        theirs.append(jnp.where(core == 0, second, first))
    mine = jnp.concatenate(mine, axis=1) if len(mine) > 1 else mine[0]
    theirs = jnp.concatenate(theirs, axis=1) if len(theirs) > 1 else theirs[0]
    other = swap_core(theirs.astype(bf16))
    return mine + other.astype(f32)


def split_rows(grads):
    core = lax.axis_index("c")
    mine, theirs = [], []
    for grad in grads:
        own = grad.shape[0] // 128
        parts = grad.reshape(16, 4, 2, own, grad.shape[1])
        first = parts[:, :, 0].reshape(16, 4 * own, grad.shape[1])
        second = parts[:, :, 1].reshape(16, 4 * own, grad.shape[1])
        mine.append(jnp.where(core == 0, first, second))
        theirs.append(jnp.where(core == 0, second, first))
    mine = jnp.concatenate(mine, axis=1)
    theirs = jnp.concatenate(theirs, axis=1)
    other = swap_core(theirs.astype(bf16))
    return mine + other.astype(f32)


def spread(value, axes):
    return lax.all_to_all(value, axes, split_axis=0, concat_axis=0, tiled=True)


def high_low(value):
    high = value.astype(bf16)
    low = (value - high.astype(f32)).astype(bf16)
    return high, low


def body(
    tokens,
    starts,
    query_weight,
    key_weight,
    value_weight,
    output_weight,
    gate_weight,
    up_weight,
    down_weight,
    input_gain,
    query_gain,
    key_gain,
    attn_gain,
    ffn_gain,
    ffn_out_gain,
    cotangent,
):
    span, width = tokens.shape
    head_dim = key_weight.shape[1]
    heads = query_weight.shape[1] // head_dim
    hq = heads * head_dim
    ff = gate_weight.shape[1]
    devices = lax.axis_size(ALL)
    hops = max(1, WINDOW // span)
    extent = hops * span + span
    scale = 1.0 / math.sqrt(head_dim)
    columns = jnp.concatenate([query_weight, key_weight, value_weight, gate_weight, up_weight], axis=1)
    rows = columns.shape[0]
    columns = jnp.pad(columns, ((0, 8 - rows), (0, 0)))
    packed = jnp.concatenate([columns, output_weight, down_weight[:8], down_weight[8:]], axis=1)
    gathered = lax.all_gather(packed, ALL, axis=0, tiled=False)
    wide = columns.shape[1]
    full_columns = gathered[:, :rows, :wide].reshape(devices * rows, wide)
    full_query = full_columns[:, :hq]
    full_key = full_columns[:, hq : hq + head_dim]
    full_value = full_columns[:, hq + head_dim : hq + 2 * head_dim]
    full_gate = full_columns[:, hq + 2 * head_dim : hq + 2 * head_dim + ff]
    full_up = full_columns[:, hq + 2 * head_dim + ff :]
    full_output = gathered[:, :, wide : wide + width].reshape(devices * 8, width)
    full_down = jnp.concatenate(
        [gathered[:, :, wide + width : wide + 2 * width], gathered[:, :, wide + 2 * width :]], axis=1
    ).reshape(devices * 16, width)

    group = lax.axis_index(ALL)
    group_ids = jnp.arange(starts.shape[0], dtype=jnp.int32)
    first_group = jnp.max(jnp.where((group_ids <= group) & (starts == 1), group_ids, 0))
    seq_first = first_group * span
    query_global = group * span + jnp.arange(span, dtype=jnp.int32)
    position = query_global - seq_first
    x_float = tokens.astype(jnp.float32)
    normed_in = rms_scale(x_float, input_gain).astype(bf16)
    query_pre = product(normed_in, full_query).reshape(span, heads, head_dim)
    key_pre = product(normed_in, full_key).reshape(span, 1, head_dim)
    value_bf = product(normed_in, full_value).astype(bf16)
    cosine, sine = rope_tables(position, head_dim)
    prepare = partial(head_prep, cosine=cosine, sine=sine)
    query_bf = prepare(query_pre, query_gain).astype(bf16)
    key_bf = prepare(key_pre, key_gain).astype(bf16).reshape(span, head_dim)
    pair = jnp.concatenate([key_bf, value_bf], axis=1)
    received = [shifted(pair, step) for step in range(hops, 0, -1)]
    both_all = jnp.concatenate(received + [pair], axis=0)
    keys_all = both_all[:, :head_dim]
    values_all = both_all[:, head_dim:]
    key_global = group * span - hops * span + jnp.arange(extent, dtype=jnp.int32)
    offset = query_global[:, None] - key_global[None, :]
    valid = (offset >= 0) & (offset < WINDOW) & (key_global[None, :] >= seq_first)
    query_flat = query_bf.reshape(span * heads, head_dim)
    scores = (transposed_right(query_flat, keys_all) * scale).reshape(span, heads, extent)
    scores = jnp.where(valid[:, None, :], scores, -1e30)
    peak = jnp.max(scores, axis=-1, keepdims=True)
    log_total = peak + jnp.log(jnp.sum(jnp.exp(scores - peak), axis=-1, keepdims=True))
    probs = jnp.exp(scores - log_total).reshape(span * heads, extent)
    probs_bf = probs.astype(bf16)
    attended_bf = product(probs_bf, values_all).reshape(span, heads * head_dim).astype(bf16)
    projected = product(attended_bf, full_output)
    resid = x_float + rms_scale(projected, attn_gain)
    normed_ffn = rms_scale(resid, ffn_gain).astype(bf16)
    gate = product(normed_ffn, full_gate)
    upward = product(normed_ffn, full_up)
    mixed_bf = gated(gate, upward).astype(bf16)
    down = product(mixed_bf, full_down)
    output = resid + rms_scale(down, ffn_out_gain)
    out_grad = cotangent.astype(jnp.float32)
    d_down, grad_ffn_out = jax.vjp(rms_scale, down, ffn_out_gain)[1](out_grad)
    d_down_bf = d_down.astype(bf16)
    grad_down = transposed_left(mixed_bf, d_down_bf)
    d_mixed = transposed_right(d_down_bf, full_down)
    d_gate, d_upward = jax.vjp(gated, gate, upward)[1](d_mixed)
    d_gate_bf = d_gate.astype(bf16)
    d_upward_bf = d_upward.astype(bf16)
    grad_gate = transposed_left(normed_ffn, d_gate_bf)
    grad_up = transposed_left(normed_ffn, d_upward_bf)
    part = split_columns([grad_gate, grad_up]).astype(bf16)
    ffn_near = jnp.sum(
        spread(part, ("y", "x")).reshape(16, -1, part.shape[1]).astype(f32), axis=0
    )
    d_normed_ffn = transposed_right(d_gate_bf, full_gate) + transposed_right(d_upward_bf, full_up)
    d_resid_part, grad_ffn = jax.vjp(rms_scale, resid, ffn_gain)[1](d_normed_ffn)
    d_resid = out_grad + d_resid_part
    d_projected, grad_attn = jax.vjp(rms_scale, projected, attn_gain)[1](d_resid)
    d_projected_bf = d_projected.astype(bf16)
    grad_output = transposed_left(attended_bf, d_projected_bf)
    part = split_rows([grad_output, grad_down]).astype(bf16)
    row_near = jnp.sum(spread(part, ("y", "x")).astype(f32), axis=0)
    d_attended_bf = transposed_right(d_projected_bf, full_output).astype(bf16)
    d_attended_bf = d_attended_bf.reshape(span * heads, head_dim)
    d_probs = transposed_right(d_attended_bf, values_all)
    balance = jnp.sum(d_probs * probs, axis=-1, keepdims=True)
    d_scores_bf = (probs * (d_probs - balance)).astype(bf16)
    d_query_bf = (
        (product(d_scores_bf, keys_all) * scale).astype(bf16).reshape(span, heads, head_dim)
    )
    d_keys_all = transposed_left(d_scores_bf, query_flat) * scale
    d_values_all = transposed_left(probs_bf, d_attended_bf)
    d_both_all = jnp.concatenate([d_keys_all, d_values_all], axis=1)
    d_both = d_both_all[hops * span :]
    for step in range(1, hops + 1):
        begin = (hops - step) * span
        d_both = d_both + shifted(d_both_all[begin : begin + span].astype(bf16), -step).astype(f32)
    d_key_bf = d_both[:, :head_dim].astype(bf16)
    d_value_bf = d_both[:, head_dim:].astype(bf16)
    d_key_pre, grad_key_gain = jax.vjp(prepare, key_pre, key_gain)[1](
        d_key_bf.astype(jnp.float32).reshape(span, 1, head_dim)
    )
    d_key_pre_bf = d_key_pre.reshape(span, head_dim).astype(bf16)
    d_query_pre, grad_query_gain = jax.vjp(prepare, query_pre, query_gain)[1](
        d_query_bf.astype(jnp.float32)
    )
    d_query_pre_bf = d_query_pre.reshape(span, heads * head_dim).astype(bf16)
    grad_query = transposed_left(normed_in, d_query_pre_bf)
    grad_key = transposed_left(normed_in, d_key_pre_bf)
    grad_value = transposed_left(normed_in, d_value_bf)
    d_normed_in = (
        transposed_right(d_query_pre_bf, full_query)
        + transposed_right(d_key_pre_bf, full_key)
        + transposed_right(d_value_bf, full_value)
    )
    d_input_part, grad_input = jax.vjp(rms_scale, x_float, input_gain)[1](d_normed_in)
    input_grad = (d_resid + d_input_part).astype(bf16)

    gains = jnp.concatenate(
        [grad_input, grad_query_gain, grad_key_gain, grad_attn, grad_ffn, grad_ffn_out]
    ).reshape(4, -1)
    part = split_columns([grad_query, grad_key, grad_value]).astype(bf16)
    part = part.reshape(16, -1, part.shape[1])
    carried = jnp.concatenate(high_low(gains), axis=0)
    part = jnp.concatenate([part, jnp.broadcast_to(carried, (16,) + carried.shape)], axis=1)
    near = jnp.sum(spread(part, ("y", "x")).astype(f32), axis=0)
    kept = near.shape[0] - 8
    gains = near[kept : kept + 4] + near[kept + 4 :]
    columns = jnp.concatenate([near[:kept], ffn_near], axis=1).astype(bf16)
    columns = jnp.pad(columns.reshape(8, rows, -1), ((0, 0), (0, 8 - rows), (0, 0)))
    carried = jnp.concatenate(high_low(gains), axis=0)
    carried = jnp.broadcast_to(carried, (8,) + carried.shape)
    own = jnp.arange(2).reshape(1, 2, 1, 1) == lax.axis_index("c")
    out_rows = row_near[: 4 * 8].reshape(4, 1, 8, width)
    down_rows = row_near[4 * 8 :].reshape(4, 1, 2, 8, width)
    row_part = jnp.concatenate([out_rows, down_rows[:, :, 0], down_rows[:, :, 1]], axis=3)
    row_part = jnp.where(own, row_part, 0.0).astype(bf16).reshape(8, 8, 3 * width)
    last = jnp.concatenate([columns, row_part, carried], axis=2)
    arrived = spread(last, ("z", "c")).astype(f32).reshape(4, 2, 8, last.shape[2]).sum(axis=0)
    near_wide = columns.shape[2]
    both = arrived[:, :rows, :near_wide]
    sizes = [hq // 2, head_dim // 2, head_dim // 2, ff // 2, ff // 2]
    column_grads, begin = [], 0
    for size in sizes:
        piece = both[:, :, begin : begin + size]
        column_grads.append(jnp.concatenate([piece[0], piece[1]], axis=1))
        begin += size
    both = arrived.sum(axis=0)
    sum_output = both[:, near_wide : near_wide + width]
    sum_down = jnp.concatenate(
        [both[:, near_wide + width : near_wide + 2 * width], both[:, near_wide + 2 * width : near_wide + 3 * width]],
        axis=0,
    )
    gains = both[:, near_wide + 3 * width :]
    gains = (gains[:4] + gains[4:]).reshape(-1)
    outs, begin = [], 0
    for size in (width, head_dim, head_dim, width, width, width):
        outs.append(gains[begin : begin + size])
        begin += size
    return (
        output.astype(bf16),
        input_grad,
        column_grads[0],
        column_grads[1],
        column_grads[2],
        sum_output,
        column_grads[3],
        column_grads[4],
        sum_down,
        *outs,
    )


def solution(mesh):
    inner = Mesh(mesh.devices.reshape(4, 4, 4, 2), ALL)
    split = P(ALL, None)
    return jax.shard_map(
        body,
        mesh=inner,
        in_specs=(split, P()) + (split,) * 7 + (P(),) * 6 + (split,),
        out_specs=(split,) * 9 + (P(),) * 6,
        check_vma=False,
    )
```

```python
from functools import partial
import math

import jax
import jax.numpy as jnp
from jax import lax
from jax.experimental import pallas as pl
from jax.experimental.pallas import tpu as pltpu
from jax.sharding import Mesh, PartitionSpec as P

WINDOW = 512
ALL = ("y", "x", "z", "c")

norm_epsilon = 1e-06
rope_base = 10000.0
GELU_A = math.sqrt(2.0 / math.pi)
GELU_B = 0.044715
bf16 = jnp.bfloat16
f32 = jnp.float32


def shifted(value, steps):
    count = lax.axis_size(ALL)
    leading, last = (max(0, -steps), min(count, count - steps))
    return lax.ppermute(value, ALL, [(source, source + steps) for source in range(leading, last)])


def rms_scale(values, gain):
    mean_square = jnp.mean(values * values, axis=-1, keepdims=True)
    return values * lax.rsqrt(mean_square + norm_epsilon) * gain


def rope_tables(position, head_dim):
    half = head_dim // 2
    exponent = jnp.arange(half, dtype=jnp.float32) * (2.0 / head_dim)
    inverse = jnp.power(jnp.float32(rope_base), -exponent)
    angles = position.astype(jnp.float32)[:, None] * inverse[None, :]
    return (jnp.cos(angles)[:, None, :], jnp.sin(angles)[:, None, :])


def head_prep(pre, gain, cosine, sine):
    normed = rms_scale(pre, gain)
    half = normed.shape[-1] // 2
    first = normed[..., :half]
    second = normed[..., half:]
    return jnp.concatenate(
        [first * cosine - second * sine, second * cosine + first * sine], axis=-1
    )


def gated(gate, upward):
    return jax.nn.gelu(gate, approximate=True) * upward


def product(left, right):
    return jnp.dot(left, right, preferred_element_type=jnp.float32)


def transposed_left(left, right):
    return lax.dot_general(
        left, right, (((0,), (0,)), ((), ())), preferred_element_type=jnp.float32
    )


def transposed_right(left, right):
    return lax.dot_general(
        left, right, (((1,), (1,)), ((), ())), preferred_element_type=jnp.float32
    )


def swap_core(value):
    return lax.ppermute(value, "c", [(0, 1), (1, 0)])


def halves(value, axis):
    core = lax.axis_index("c")
    mine = lax.dynamic_index_in_dim(value, core, axis, keepdims=False)
    theirs = lax.dynamic_index_in_dim(value, 1 - core, axis, keepdims=False)
    return mine, theirs


def core_sum(value, axis):
    mine, theirs = halves(value.astype(bf16), axis)
    return (mine.astype(f32) + swap_core(theirs).astype(f32)).astype(bf16)


def chosen(rows, source):
    return (jnp.arange(rows, dtype=jnp.int32)[:, None] == source[None, :]).astype(bf16)


def spread(value, axes):
    return lax.all_to_all(value, axes, split_axis=0, concat_axis=0, tiled=True)


def high_low(value):
    high = value.astype(bf16)
    low = (value - high.astype(f32)).astype(bf16)
    return high, low


def rms_inverse(values):
    return lax.rsqrt(jnp.mean(values * values, axis=-1, keepdims=True) + norm_epsilon)


def rms_back(values, inverse, gain, grad):
    scaled = grad * gain
    kept = values * inverse
    back = inverse * (scaled - kept * jnp.mean(scaled * kept, axis=-1, keepdims=True))
    return back, jnp.sum(grad * kept, axis=0, keepdims=True)


def one_hot(source, count):
    return (lax.broadcasted_iota(jnp.int32, (count, source.shape[1]), 0) == source).astype(f32).astype(bf16)


CHUNK = 512


def ffn_kernel(
    attended, tokens, cotangent, gathered, attn_gain, ffn_gain, out_gain, pad_source, last_source,
    output, grad_down, grad_wide, grad_output, d_resid, d_attended, gains,
    wide, low, first, second, mixed, normed_pad, normed_turned, projected, resid, pad_rows, d_down, down, d_pad, sems,
):
    span, width = tokens.shape
    ff = mixed.shape[1]
    steps = ff // CHUNK
    copies = [pltpu.make_async_copy(gathered.at[:, 2 * ff :], low, sems.at[0])]
    for step in range(2 * steps):
        part = pl.ds((step // 2) * CHUNK + (step % 2) * ff, CHUNK)
        copies.append(pltpu.make_async_copy(gathered.at[:, part], wide.at[:, part], sems.at[1 + step]))
    for copy in copies:
        copy.start()
    pad_rows[...] = one_hot(pad_source[...], width)
    copies[0].wait()
    projected[...] = product(attended[...], low[:, :width])
    value = projected[...]
    resid[...] = tokens[...].astype(f32) + value * rms_inverse(value) * attn_gain[...]
    value = resid[...]
    normed = (value * rms_inverse(value) * ffn_gain[...]).astype(bf16)
    normed_pad[...] = product(normed, pad_rows[...]).astype(bf16)
    normed_turned[...] = product(normed, one_hot(last_source[...], width)).astype(bf16).T
    down[...] = jnp.zeros_like(down)

    def down_part(step):
        block = pl.ds(pl.multiple_of(step * (CHUNK // 2), CHUNK // 2), CHUNK // 2)
        parts = [low[block, begin : begin + width].astype(f32).reshape(CHUNK // 16, 8, width) for begin in (width, 2 * width)]
        return jnp.concatenate(parts, axis=1).reshape(CHUNK, width).astype(bf16)

    for step in range(steps):
        here = pl.ds(step * CHUNK, CHUNK)
        there = pl.ds(ff + step * CHUNK, CHUNK)
        copies[1 + 2 * step].wait()
        copies[2 + 2 * step].wait()
        gate = product(normed_pad[...], wide[:, here])
        upward = product(normed_pad[...], wide[:, there])
        square = gate * gate
        bend = jnp.tanh(gate * (GELU_A + GELU_A * GELU_B * square))
        half = 0.5 + 0.5 * bend
        curve = gate * half
        slope = half + 0.5 * gate * (1.0 - bend * bend) * (GELU_A + 3.0 * GELU_A * GELU_B * square)
        first[:, here] = curve
        second[:, here] = slope * upward
        mixed[:, here] = (curve * upward).astype(bf16)
        down[...] += product(mixed[:, here], down_part(step))

    value = down[...]
    inverse = rms_inverse(value)
    output[...] = (resid[...] + value * inverse * out_gain[...]).astype(bf16)
    back, gains[0:1, :] = rms_back(value, inverse, out_gain[...], cotangent[...].astype(f32))
    d_down[...] = back.astype(bf16)
    d_pad[...] = jnp.zeros_like(d_pad)
    for step in range(steps):
        here = pl.ds(step * CHUNK, CHUNK)
        there = pl.ds(ff + step * CHUNK, CHUNK)
        grad_down[here, :] = transposed_left(mixed[:, here], d_down[...]).astype(bf16)
        d_mixed = transposed_right(d_down[...], down_part(step))
        d_gate = (d_mixed * second[:, here]).astype(bf16)
        d_upward = (d_mixed * first[:, here]).astype(bf16)
        grad_wide[:, here] = product(normed_turned[...], d_gate).astype(bf16)
        grad_wide[:, there] = product(normed_turned[...], d_upward).astype(bf16)
        d_pad[...] += transposed_right(d_gate, wide[:, here]) + transposed_right(d_upward, wide[:, there])
    high, lower = high_low(d_pad[...])
    d_normed = transposed_right(high, pad_rows[...]) + transposed_right(lower, pad_rows[...])
    value = resid[...]
    back, gains[1:2, :] = rms_back(value, rms_inverse(value), ffn_gain[...], d_normed)
    back = cotangent[...].astype(f32) + back
    d_resid[...] = back
    value = projected[...]
    back, gains[2:3, :] = rms_back(value, rms_inverse(value), attn_gain[...], back)
    back = back.astype(bf16)
    grad_output[...] = transposed_left(attended[...], back).astype(bf16)
    d_attended[...] = transposed_right(back, low[:, :width]).astype(bf16)


def ffn(attended, tokens, cotangent, gathered, attn_gain, ffn_gain, out_gain, pad_source, last_source):
    span, width = tokens.shape
    hq = attended.shape[1]
    ff = (gathered.shape[1] - 3 * width) // 2
    padded, spaced = gathered.shape[0], last_source.shape[0]
    vmem = pl.BlockSpec(memory_space=pltpu.VMEM)
    shape = jax.ShapeDtypeStruct
    return pl.pallas_call(
        ffn_kernel,
        out_shape=(
            shape((span, width), bf16),
            shape((ff, width), bf16),
            shape((spaced, 2 * ff), bf16),
            shape((hq, width), bf16),
            shape((span, width), f32),
            shape((span, hq), bf16),
            shape((3, width), f32),
        ),
        in_specs=[vmem] * 3 + [pl.BlockSpec(memory_space=pl.ANY)] + [vmem] * 5,
        out_specs=(vmem,) * 7,
        scratch_shapes=[
            pltpu.VMEM((padded, 2 * ff), bf16),
            pltpu.VMEM((padded, 3 * width), bf16),
            pltpu.VMEM((span, ff), f32),
            pltpu.VMEM((span, ff), f32),
            pltpu.VMEM((span, ff), bf16),
            pltpu.VMEM((span, padded), bf16),
            pltpu.VMEM((spaced, span), bf16),
            pltpu.VMEM((span, width), f32),
            pltpu.VMEM((span, width), f32),
            pltpu.VMEM((width, padded), bf16),
            pltpu.VMEM((span, width), bf16),
            pltpu.VMEM((span, width), f32),
            pltpu.VMEM((span, padded), f32),
            pltpu.SemaphoreType.DMA((1 + 2 * (ff // CHUNK),)),
        ],
        compiler_params=pltpu.CompilerParams(vmem_limit_bytes=56 * 1024 * 1024),
        cost_estimate=pl.CostEstimate(flops=9 * 10**9, bytes_accessed=24 * 2**20, transcendentals=span * ff),
        name="ffn",
    )(
        attended, tokens, cotangent, gathered, attn_gain[None], ffn_gain[None], out_gain[None],
        pad_source[None], last_source[None],
    )


def body(
    tokens,
    starts,
    query_weight,
    key_weight,
    value_weight,
    output_weight,
    gate_weight,
    up_weight,
    down_weight,
    input_gain,
    query_gain,
    key_gain,
    attn_gain,
    ffn_gain,
    ffn_out_gain,
    cotangent,
):
    span, width = tokens.shape
    head_dim = key_weight.shape[1]
    heads = query_weight.shape[1] // head_dim
    hq = heads * head_dim
    ff = gate_weight.shape[1]
    devices = lax.axis_size(ALL)
    hops = max(1, WINDOW // span)
    extent = hops * span + span
    scale = 1.0 / math.sqrt(head_dim)
    core = lax.axis_index("c")
    rows = query_weight.shape[0]
    columns = jnp.concatenate([gate_weight, up_weight], axis=1)
    columns = jnp.pad(columns, ((0, 8 - rows), (0, 0)))
    packed = jnp.concatenate([columns, output_weight, down_weight[:8], down_weight[8:]], axis=1)
    gathered = lax.all_gather(packed, ALL, axis=0, tiled=True)
    qkv = jnp.concatenate([query_weight, key_weight, value_weight], axis=1)
    qkv = lax.all_gather(jnp.pad(qkv, ((0, 8 - rows), (0, 0))), ("z", "c"), axis=0, tiled=False)
    qkv = qkv[:, :rows].reshape(8 * rows, -1)
    qkv = jnp.concatenate(
        [
            lax.dynamic_slice_in_dim(part, core * (part.shape[1] // 2), part.shape[1] // 2, 1)
            for part in (qkv[:, :hq], qkv[:, hq : hq + head_dim], qkv[:, hq + head_dim :])
        ],
        axis=1,
    )
    qkv = spread(jnp.broadcast_to(qkv, (16,) + qkv.shape), ("y", "x")).reshape(16 * 8 * rows, -1)
    other = swap_core(qkv)
    left = jnp.where(core == 0, qkv, other)
    right = jnp.where(core == 0, other, qkv)
    half, small = hq // 2, head_dim // 2
    full_query = jnp.concatenate([left[:, :half], right[:, :half]], axis=1)
    full_key = jnp.concatenate([left[:, half : half + small], right[:, half : half + small]], axis=1)
    full_value = jnp.concatenate([left[:, half + small :], right[:, half + small :]], axis=1)

    place = jnp.arange(devices * 8, dtype=jnp.int32)
    pad_source = jnp.where(place % 8 < rows, place // 8 * rows + place % 8, -1)
    place = jnp.arange(2 * 16 * 24, dtype=jnp.int32)
    zr, x, y, c = place % 24, place // 24 % 4, place // (24 * 4) % 4, place // (24 * 16)
    last_source = jnp.where(zr < 4 * rows, (((y * 4 + x) * 4 + zr // rows) * 2 + c) * rows + zr % rows, -1)
    order_last = chosen(width, last_source)

    group = lax.axis_index(ALL)
    group_ids = jnp.arange(starts.shape[0], dtype=jnp.int32)
    first_group = jnp.max(jnp.where((group_ids <= group) & (starts == 1), group_ids, 0))
    seq_first = first_group * span
    query_global = group * span + jnp.arange(span, dtype=jnp.int32)
    position = query_global - seq_first
    x_float = tokens.astype(jnp.float32)
    normed_in = rms_scale(x_float, input_gain).astype(bf16)
    query_pre = product(normed_in, full_query).reshape(span, heads, head_dim)
    key_pre = product(normed_in, full_key).reshape(span, 1, head_dim)
    value_bf = product(normed_in, full_value).astype(bf16)
    cosine, sine = rope_tables(position, head_dim)
    prepare = partial(head_prep, cosine=cosine, sine=sine)
    query_bf = prepare(query_pre, query_gain).astype(bf16)
    key_bf = prepare(key_pre, key_gain).astype(bf16).reshape(span, head_dim)
    pair = jnp.concatenate([key_bf, value_bf], axis=1)
    received = [shifted(pair, step) for step in range(hops, 0, -1)]
    both_all = jnp.concatenate(received + [pair], axis=0)
    keys_all = both_all[:, :head_dim]
    values_all = both_all[:, head_dim:]
    key_global = group * span - hops * span + jnp.arange(extent, dtype=jnp.int32)
    offset = query_global[:, None] - key_global[None, :]
    valid = (offset >= 0) & (offset < WINDOW) & (key_global[None, :] >= seq_first)
    query_flat = query_bf.reshape(span * heads, head_dim)
    scores = (transposed_right(query_flat, keys_all) * scale).reshape(span, heads, extent)
    scores = jnp.where(valid[:, None, :], scores, -1e30)
    peak = jnp.max(scores, axis=-1, keepdims=True)
    log_total = peak + jnp.log(jnp.sum(jnp.exp(scores - peak), axis=-1, keepdims=True))
    probs = jnp.exp(scores - log_total).reshape(span * heads, extent)
    probs_bf = probs.astype(bf16)
    attended_bf = product(probs_bf, values_all).reshape(span, heads * head_dim).astype(bf16)
    output, grad_down, grads_wide, grad_output, d_resid, d_attended_bf, ffn_gains = ffn(
        attended_bf, tokens, cotangent, gathered, attn_gain, ffn_gain, ffn_out_gain, pad_source, last_source
    )
    wide = lax.psum_scatter(grads_wide, "c", scatter_dimension=0, tiled=True)
    wide = lax.psum_scatter(wide, "y", scatter_dimension=0, tiled=True)
    wide = lax.psum_scatter(wide, "x", scatter_dimension=0, tiled=True)
    part_low = core_sum(
        jnp.concatenate(
            [grad_output.reshape(16, 4, 2, 8, width), grad_down.reshape(16, 4, 2, 16, width)], axis=3
        ),
        2,
    )
    near_low = spread(part_low.reshape(16, 4 * 24, width), ("y", "x"))
    d_attended_bf = d_attended_bf.reshape(span * heads, head_dim)
    d_probs = transposed_right(d_attended_bf, values_all)
    balance = jnp.sum(d_probs * probs, axis=-1, keepdims=True)
    d_scores_bf = (probs * (d_probs - balance)).astype(bf16)
    d_keys_all = transposed_left(d_scores_bf, query_flat) * scale
    d_values_all = transposed_left(probs_bf, d_attended_bf)
    d_both_all = jnp.concatenate([d_keys_all, d_values_all], axis=1)
    d_both = d_both_all[hops * span :]
    for step in range(1, hops + 1):
        begin = (hops - step) * span
        d_both = d_both + shifted(d_both_all[begin : begin + span].astype(bf16), -step).astype(f32)
    d_query_bf = (
        (product(d_scores_bf, keys_all) * scale).astype(bf16).reshape(span, heads, head_dim)
    )
    d_key_bf = d_both[:, :head_dim].astype(bf16)
    d_value_bf = d_both[:, head_dim:].astype(bf16)
    d_key_pre, grad_key_gain = jax.vjp(prepare, key_pre, key_gain)[1](
        d_key_bf.astype(jnp.float32).reshape(span, 1, head_dim)
    )
    d_key_pre_bf = d_key_pre.reshape(span, head_dim).astype(bf16)
    d_query_pre, grad_query_gain = jax.vjp(prepare, query_pre, query_gain)[1](
        d_query_bf.astype(jnp.float32)
    )
    d_query_pre_bf = d_query_pre.reshape(span, heads * head_dim).astype(bf16)
    d_qkv = jnp.concatenate([d_query_pre_bf, d_key_pre_bf, d_value_bf], axis=1)
    normed_last = product(normed_in, order_last).astype(bf16)
    grads = transposed_left(normed_last, d_qkv)
    part_qkv = core_sum(grads.reshape(2, 16, 24, -1), 0)
    d_normed_in = (
        transposed_right(d_query_pre_bf, full_query)
        + transposed_right(d_key_pre_bf, full_key)
        + transposed_right(d_value_bf, full_value)
    )
    d_input_part, grad_input = jax.vjp(rms_scale, x_float, input_gain)[1](d_normed_in)
    input_grad = (d_resid + d_input_part).astype(bf16)

    gains = jnp.concatenate(
        [grad_input, grad_query_gain, grad_key_gain, ffn_gains[2], ffn_gains[1], ffn_gains[0]]
    ).reshape(2, -1)
    gains = gains + swap_core(gains)
    carried = jnp.concatenate(high_low(gains), axis=0)
    part_qkv = jnp.concatenate(
        [part_qkv[:, : 4 * rows], jnp.broadcast_to(carried, (16,) + carried.shape)], axis=1
    )
    near_qkv = jnp.sum(spread(part_qkv, ("y", "x")).astype(f32), axis=0)
    gains = (near_qkv[4 * rows : 4 * rows + 2] + near_qkv[4 * rows + 2 :]).reshape(4, -1)
    carried = jnp.concatenate(high_low(gains), axis=0)
    low = jnp.sum(near_low.astype(f32), axis=0).astype(bf16).reshape(4, 3, 8, width)
    low_columns = jnp.concatenate([near_qkv[: 4 * rows].astype(bf16), wide[: 4 * rows]], axis=1)
    low_columns = jnp.pad(low_columns.reshape(4, rows, -1), ((0, 0), (0, 8 - rows), (0, 0)))
    last = jnp.concatenate(
        [low_columns, low[:, 0], low[:, 1], low[:, 2], jnp.broadcast_to(carried, (4,) + carried.shape)],
        axis=2,
    )
    last = jnp.sum(spread(last, "z").astype(f32), axis=0)
    begin = hq + 2 * head_dim
    sum_qkv = last[:rows, :begin]
    sum_gate = last[:rows, begin : begin + ff]
    sum_up = last[:rows, begin + ff : begin + 2 * ff]
    begin += 2 * ff
    sum_output = last[:, begin : begin + width]
    begin += width
    sum_down = jnp.concatenate([last[:, begin : begin + width], last[:, begin + width : begin + 2 * width]], axis=0)
    gains = last[:, begin + 2 * width :]
    gains = (gains[:4] + gains[4:]).reshape(-1)
    outs, begin = [], 0
    for size in (width, head_dim, head_dim, width, width, width):
        outs.append(gains[begin : begin + size])
        begin += size
    return (
        output,
        input_grad,
        sum_qkv[:, :hq],
        sum_qkv[:, hq : hq + head_dim],
        sum_qkv[:, hq + head_dim :],
        sum_output,
        sum_gate,
        sum_up,
        sum_down,
        *outs,
    )


def solution(mesh):
    inner = Mesh(mesh.devices.reshape(4, 4, 4, 2), ALL)
    split = P(ALL, None)
    return jax.shard_map(
        body,
        mesh=inner,
        in_specs=(split, P()) + (split,) * 7 + (P(),) * 6 + (split,),
        out_specs=(split,) * 9 + (P(),) * 6,
        check_vma=False,
    )
```

```python
from functools import partial
import math

import jax
import jax.numpy as jnp
from jax import lax
from jax.experimental import pallas as pl
from jax.experimental.pallas import tpu as pltpu
from jax.sharding import Mesh, PartitionSpec as P

WINDOW = 512
ALL = ("y", "x", "z", "c")

norm_epsilon = 1e-06
rope_base = 10000.0
GELU_A = math.sqrt(2.0 / math.pi)
GELU_B = 0.044715
bf16 = jnp.bfloat16
f32 = jnp.float32


def shifted(value, steps):
    count = lax.axis_size(ALL)
    leading, last = (max(0, -steps), min(count, count - steps))
    return lax.ppermute(value, ALL, [(source, source + steps) for source in range(leading, last)])


def rms_scale(values, gain):
    mean_square = jnp.mean(values * values, axis=-1, keepdims=True)
    return values * lax.rsqrt(mean_square + norm_epsilon) * gain


def rope_tables(position, head_dim):
    half = head_dim // 2
    exponent = jnp.arange(half, dtype=jnp.float32) * (2.0 / head_dim)
    inverse = jnp.power(jnp.float32(rope_base), -exponent)
    angles = position.astype(jnp.float32)[:, None] * inverse[None, :]
    return (jnp.cos(angles)[:, None, :], jnp.sin(angles)[:, None, :])


def head_prep(pre, gain, cosine, sine):
    normed = rms_scale(pre, gain)
    half = normed.shape[-1] // 2
    first = normed[..., :half]
    second = normed[..., half:]
    return jnp.concatenate(
        [first * cosine - second * sine, second * cosine + first * sine], axis=-1
    )


def gated(gate, upward):
    return jax.nn.gelu(gate, approximate=True) * upward


def product(left, right):
    return jnp.dot(left, right, preferred_element_type=jnp.float32)


def transposed_left(left, right):
    return lax.dot_general(
        left, right, (((0,), (0,)), ((), ())), preferred_element_type=jnp.float32
    )


def transposed_right(left, right):
    return lax.dot_general(
        left, right, (((1,), (1,)), ((), ())), preferred_element_type=jnp.float32
    )


def swap_core(value):
    return lax.ppermute(value, "c", [(0, 1), (1, 0)])


def halves(value, axis):
    core = lax.axis_index("c")
    mine = lax.dynamic_index_in_dim(value, core, axis, keepdims=False)
    theirs = lax.dynamic_index_in_dim(value, 1 - core, axis, keepdims=False)
    return mine, theirs


def core_sum(value, axis):
    mine, theirs = halves(value.astype(bf16), axis)
    return (mine.astype(f32) + swap_core(theirs).astype(f32)).astype(bf16)


def chosen(rows, source):
    return (jnp.arange(rows, dtype=jnp.int32)[:, None] == source[None, :]).astype(bf16)


def spread(value, axes):
    return lax.all_to_all(value, axes, split_axis=0, concat_axis=0, tiled=True)


def ring_sum(blocks, axis):
    place = lax.axis_index(axis)
    total = lax.dynamic_index_in_dim(blocks, place, 0, keepdims=False).astype(f32)
    for step in (1, 3, 2):
        block = lax.dynamic_index_in_dim(blocks, lax.rem(place + step, 4), 0, keepdims=False)
        total = total + lax.ppermute(block, axis, [(i, (i + step) % 4) for i in range(4)]).astype(f32)
    return total


def high_low(value):
    high = value.astype(bf16)
    low = (value - high.astype(f32)).astype(bf16)
    return high, low


def rms_inverse(values):
    return lax.rsqrt(jnp.mean(values * values, axis=-1, keepdims=True) + norm_epsilon)


def rms_back(values, inverse, gain, grad):
    scaled = grad * gain
    kept = values * inverse
    back = inverse * (scaled - kept * jnp.mean(scaled * kept, axis=-1, keepdims=True))
    return back, jnp.sum(grad * kept, axis=0, keepdims=True)


def one_hot(source, count):
    return (lax.broadcasted_iota(jnp.int32, (count, source.shape[1]), 0) == source).astype(f32).astype(bf16)


CHUNK = 512


def ffn_kernel(
    core, attended, tokens, cotangent, gathered, attn_gain, ffn_gain, out_gain, pad_source, last_source,
    output, grad_own, grad_other, grad_wide, d_resid, d_attended, gains,
    grad_low, wide, low, first, second, mixed, normed_pad, normed_turned, projected, resid, pad_rows, d_down, down, d_pad, sems,
):
    span, width = tokens.shape
    ff = mixed.shape[1]
    steps = ff // CHUNK
    copies = [pltpu.make_async_copy(gathered.at[:, 2 * ff :], low, sems.at[0])]
    for step in range(2 * steps):
        part = pl.ds((step // 2) * CHUNK + (step % 2) * ff, CHUNK)
        copies.append(pltpu.make_async_copy(gathered.at[:, part], wide.at[:, part], sems.at[1 + step]))
    for copy in copies:
        copy.start()
    pad_rows[...] = one_hot(pad_source[...], width)
    copies[0].wait()
    projected[...] = product(attended[...], low[:, :width])
    value = projected[...]
    resid[...] = tokens[...].astype(f32) + value * rms_inverse(value) * attn_gain[...]
    value = resid[...]
    normed = (value * rms_inverse(value) * ffn_gain[...]).astype(bf16)
    normed_pad[...] = product(normed, pad_rows[...]).astype(bf16)
    normed_turned[...] = product(normed, one_hot(last_source[...], width)).astype(bf16).T
    down[...] = jnp.zeros_like(down)

    def down_part(step):
        block = pl.ds(pl.multiple_of(step * (CHUNK // 2), CHUNK // 2), CHUNK // 2)
        parts = [low[block, begin : begin + width].astype(f32).reshape(CHUNK // 16, 8, width) for begin in (width, 2 * width)]
        return jnp.concatenate(parts, axis=1).reshape(CHUNK, width).astype(bf16)

    for step in range(steps):
        here = pl.ds(step * CHUNK, CHUNK)
        there = pl.ds(ff + step * CHUNK, CHUNK)
        copies[1 + 2 * step].wait()
        copies[2 + 2 * step].wait()
        gate = product(normed_pad[...], wide[:, here])
        upward = product(normed_pad[...], wide[:, there])
        square = gate * gate
        bend = jnp.tanh(gate * (GELU_A + GELU_A * GELU_B * square))
        half = 0.5 + 0.5 * bend
        curve = gate * half
        slope = half + 0.5 * gate * (1.0 - bend * bend) * (GELU_A + 3.0 * GELU_A * GELU_B * square)
        first[:, here] = curve
        second[:, here] = slope * upward
        mixed[:, here] = (curve * upward).astype(bf16)
        down[...] += product(mixed[:, here], down_part(step))

    value = down[...]
    inverse = rms_inverse(value)
    output[...] = (resid[...] + value * inverse * out_gain[...]).astype(bf16)
    back, gains[0:1, :] = rms_back(value, inverse, out_gain[...], cotangent[...].astype(f32))
    d_down[...] = back.astype(bf16)
    d_pad[...] = jnp.zeros_like(d_pad)
    for step in range(steps):
        here = pl.ds(step * CHUNK, CHUNK)
        there = pl.ds(ff + step * CHUNK, CHUNK)
        grad = transposed_left(mixed[:, here], d_down[...]).astype(bf16).reshape(CHUNK // 128, 4, 2, 16, width)
        blocks = pl.ds(step * (CHUNK // 128), CHUNK // 128)
        grad_low[0, blocks, :, :16] = grad[:, :, 0]
        grad_low[1, blocks, :, :16] = grad[:, :, 1]
        d_mixed = transposed_right(d_down[...], down_part(step))
        d_gate = (d_mixed * second[:, here]).astype(bf16)
        d_upward = (d_mixed * first[:, here]).astype(bf16)
        grad_wide[:, here] = product(normed_turned[...], d_gate).astype(bf16)
        grad_wide[:, there] = product(normed_turned[...], d_upward).astype(bf16)
        d_pad[...] += transposed_right(d_gate, wide[:, here]) + transposed_right(d_upward, wide[:, there])
    out_copies = []
    for half, grad in enumerate((grad_own, grad_other)):
        source = grad_low.at[core[0] if half == 0 else 1 - core[0]]
        out_copies.append(pltpu.make_async_copy(source.at[:, :, :16], grad.at[:, :, :16], sems.at[half]))
        out_copies.append(pltpu.make_async_copy(source.at[:, :, 16:], grad.at[:, :, 16:], sems.at[2 + half]))
    out_copies[0].start()
    out_copies[2].start()
    high, lower = high_low(d_pad[...])
    d_normed = transposed_right(high, pad_rows[...]) + transposed_right(lower, pad_rows[...])
    value = resid[...]
    back, gains[1:2, :] = rms_back(value, rms_inverse(value), ffn_gain[...], d_normed)
    back = cotangent[...].astype(f32) + back
    d_resid[...] = back
    value = projected[...]
    back, gains[2:3, :] = rms_back(value, rms_inverse(value), attn_gain[...], back)
    back = back.astype(bf16)
    grad = transposed_left(attended[...], back).reshape(16, 4, 2, 8, width)
    grad_low[0, :, :, 16:] = grad[:, :, 0].astype(bf16)
    grad_low[1, :, :, 16:] = grad[:, :, 1].astype(bf16)
    out_copies[1].start()
    out_copies[3].start()
    d_attended[...] = transposed_right(back, low[:, :width]).astype(bf16)
    for copy in out_copies:
        copy.wait()


def ffn(core, attended, tokens, cotangent, gathered, attn_gain, ffn_gain, out_gain, pad_source, last_source):
    span, width = tokens.shape
    hq = attended.shape[1]
    ff = (gathered.shape[1] - 3 * width) // 2
    padded, spaced = gathered.shape[0], last_source.shape[0]
    vmem = pl.BlockSpec(memory_space=pltpu.VMEM)
    shape = jax.ShapeDtypeStruct
    return pl.pallas_call(
        ffn_kernel,
        out_shape=(
            shape((span, width), bf16),
            shape((16, 4, 24, width), bf16),
            shape((16, 4, 24, width), bf16),
            shape((spaced, 2 * ff), bf16),
            shape((span, width), f32),
            shape((span, hq), bf16),
            shape((3, width), f32),
        ),
        in_specs=[pl.BlockSpec(memory_space=pltpu.SMEM)] + [vmem] * 3 + [pl.BlockSpec(memory_space=pl.ANY)] + [vmem] * 5,
        out_specs=(vmem, pl.BlockSpec(memory_space=pl.ANY), pl.BlockSpec(memory_space=pl.ANY)) + (vmem,) * 4,
        scratch_shapes=[
            pltpu.VMEM((2, 16, 4, 24, width), bf16),
            pltpu.VMEM((padded, 2 * ff), bf16),
            pltpu.VMEM((padded, 3 * width), bf16),
            pltpu.VMEM((span, ff), f32),
            pltpu.VMEM((span, ff), f32),
            pltpu.VMEM((span, ff), bf16),
            pltpu.VMEM((span, padded), bf16),
            pltpu.VMEM((spaced, span), bf16),
            pltpu.VMEM((span, width), f32),
            pltpu.VMEM((span, width), f32),
            pltpu.VMEM((width, padded), bf16),
            pltpu.VMEM((span, width), bf16),
            pltpu.VMEM((span, width), f32),
            pltpu.VMEM((span, padded), f32),
            pltpu.SemaphoreType.DMA((1 + 2 * (ff // CHUNK),)),
        ],
        compiler_params=pltpu.CompilerParams(vmem_limit_bytes=56 * 1024 * 1024),
        cost_estimate=pl.CostEstimate(flops=9 * 10**9, bytes_accessed=24 * 2**20, transcendentals=span * ff),
        name="ffn",
    )(
        core, attended, tokens, cotangent, gathered, attn_gain[None], ffn_gain[None], out_gain[None],
        pad_source[None], last_source[None],
    )


def turn_back(grad, cosine, sine):
    half = grad.shape[1] // 2
    first, second = grad[:, :half], grad[:, half:]
    return jnp.concatenate([first * cosine + second * sine, second * cosine - first * sine], axis=1)


def attention_back_kernel(
    bound, queries, both, d_attended, query_pre, cosine, sine, query_gain,
    d_own, d_near, d_far, d_query_pre, grad_gain, d_both,
):
    span, hq = queries.shape
    extent = both.shape[0]
    head_dim = both.shape[1] // 2
    scale = 1.0 / math.sqrt(head_dim)
    offset = (
        lax.broadcasted_iota(jnp.int32, (span, extent), 0)
        - lax.broadcasted_iota(jnp.int32, (span, extent), 1)
        + (extent - span)
    )
    place = lax.broadcasted_iota(jnp.int32, (span, extent), 1)
    valid = (offset >= 0) & (offset < WINDOW) & (place >= bound[0])
    keys, values = both[:, :head_dim], both[:, head_dim:]
    gain_sum = jnp.zeros((1, head_dim), f32)
    for head in range(hq // head_dim):
        here = pl.ds(head * head_dim, head_dim)
        query, d_att = queries[:, here], d_attended[:, here]
        scores = jnp.where(valid, transposed_right(query, keys) * scale, -1e30)
        weights = jnp.exp(scores - jnp.max(scores, axis=-1, keepdims=True))
        probs = weights * (1.0 / jnp.sum(weights, axis=-1, keepdims=True))
        d_probs = transposed_right(d_att, values)
        balance = jnp.sum(d_probs * probs, axis=-1, keepdims=True)
        d_scores = (probs * (d_probs - balance)).astype(bf16)
        d_query = (product(d_scores, keys) * scale).astype(bf16).astype(f32)
        d_key = transposed_left(d_scores, query) * scale
        d_value = transposed_left(probs.astype(bf16), d_att)
        if head == 0:
            d_both[:, :head_dim] = d_key
            d_both[:, head_dim:] = d_value
        else:
            d_both[:, :head_dim] += d_key
            d_both[:, head_dim:] += d_value
        pre = query_pre[:, here]
        back, gain_part = rms_back(pre, rms_inverse(pre), query_gain[...], turn_back(d_query, cosine[...], sine[...]))
        gain_sum += gain_part
        d_query_pre[:, here] = back.astype(bf16)
    grad_gain[...] = gain_sum
    d_far[...] = d_both[:span, :].astype(bf16)
    d_near[...] = d_both[span : 2 * span, :].astype(bf16)
    d_own[...] = d_both[2 * span :, :]


def attention_back(bound, queries, both, d_attended, query_pre, cosine, sine, query_gain):
    span, hq = queries.shape
    extent, pair = both.shape
    vmem = pl.BlockSpec(memory_space=pltpu.VMEM)
    shape = jax.ShapeDtypeStruct
    return pl.pallas_call(
        attention_back_kernel,
        out_shape=(
            shape((span, pair), f32),
            shape((span, pair), bf16),
            shape((span, pair), bf16),
            shape((span, hq), bf16),
            shape((1, pair // 2), f32),
        ),
        in_specs=[pl.BlockSpec(memory_space=pltpu.SMEM)] + [vmem] * 7,
        out_specs=(vmem,) * 5,
        scratch_shapes=[pltpu.VMEM((extent, pair), f32)],
        compiler_params=pltpu.CompilerParams(vmem_limit_bytes=48 * 1024 * 1024),
        cost_estimate=pl.CostEstimate(flops=12 * span * extent * hq, bytes_accessed=6 * 2**20, transcendentals=4 * span * extent),
        name="attention_back",
    )(bound, queries, both, d_attended, query_pre, cosine, sine, query_gain[None])


def query_back_kernel(d_query_pre, normed, source, weight, grads, d_normed, turned):
    turned[...] = product(normed[...], one_hot(source[...], normed.shape[1])).astype(bf16).T
    grads[...] = product(turned[...], d_query_pre[...]).astype(bf16)
    d_normed[...] = transposed_right(d_query_pre[...], weight[...])


def query_back(d_query_pre, normed, source, weight):
    span, width = normed.shape
    vmem = pl.BlockSpec(memory_space=pltpu.VMEM)
    shape = jax.ShapeDtypeStruct
    return pl.pallas_call(
        query_back_kernel,
        out_shape=(
            shape((source.shape[0], d_query_pre.shape[1]), bf16),
            shape((span, width), f32),
            shape((source.shape[0], span), bf16),
        ),
        in_specs=[vmem] * 4,
        out_specs=(vmem,) * 3,
        compiler_params=pltpu.CompilerParams(vmem_limit_bytes=48 * 1024 * 1024),
        cost_estimate=pl.CostEstimate(flops=10**9, bytes_accessed=4 * 2**20, transcendentals=0),
        name="query_back",
    )(d_query_pre, normed, source[None], weight)


def key_back_kernel(
    d_own, d_near, d_far, key_pre, cosine, sine, key_gain, turned, key_weight, value_weight, d_normed, tokens, input_gain,
    d_resid, ffn_gains, query_gain_grad, grads, input_grad, gains,
):
    head_dim = key_pre.shape[1]
    width = tokens.shape[1]
    total = d_own[...] + d_near[...].astype(f32) + d_far[...].astype(f32)
    d_key = total[:, :head_dim].astype(bf16).astype(f32)
    d_value = total[:, head_dim:].astype(bf16)
    pre = key_pre[...]
    back, gain_part = rms_back(pre, rms_inverse(pre), key_gain[...], turn_back(d_key, cosine[...], sine[...]))
    back = back.astype(bf16)
    grads[:, :head_dim] = product(turned[...], back).astype(bf16)
    grads[:, head_dim:] = product(turned[...], d_value).astype(bf16)
    d_in = d_normed[...] + transposed_right(back, key_weight[...]) + transposed_right(d_value, value_weight[...])
    value = tokens[...].astype(f32)
    back, gain_in = rms_back(value, rms_inverse(value), input_gain[...], d_in)
    input_grad[...] = (d_resid[...] + back).astype(bf16)
    gains[:, :width] = gain_in
    gains[:, width : width + head_dim] = query_gain_grad[...]
    gains[:, width + head_dim : width + 2 * head_dim] = gain_part
    begin = width + 2 * head_dim
    for row in (2, 1, 0):
        gains[:, begin : begin + width] = ffn_gains[row : row + 1, :]
        begin += width


def key_back(
    d_own, d_near, d_far, key_pre, cosine, sine, key_gain, turned, key_weight, value_weight, d_normed, tokens, input_gain,
    d_resid, ffn_gains, query_gain_grad,
):
    span, width = tokens.shape
    head_dim = key_pre.shape[1]
    vmem = pl.BlockSpec(memory_space=pltpu.VMEM)
    shape = jax.ShapeDtypeStruct
    return pl.pallas_call(
        key_back_kernel,
        out_shape=(
            shape((turned.shape[0], 2 * head_dim), bf16),
            shape((span, width), bf16),
            shape((1, 4 * width + 2 * head_dim), f32),
        ),
        in_specs=[vmem] * 16,
        out_specs=(vmem,) * 3,
        compiler_params=pltpu.CompilerParams(vmem_limit_bytes=48 * 1024 * 1024),
        cost_estimate=pl.CostEstimate(flops=10**9, bytes_accessed=6 * 2**20, transcendentals=0),
        name="key_back",
    )(
        d_own, d_near, d_far, key_pre, cosine, sine, key_gain[None], turned, key_weight, value_weight, d_normed, tokens,
        input_gain[None], d_resid, ffn_gains, query_gain_grad,
    )


def body(
    tokens,
    starts,
    query_weight,
    key_weight,
    value_weight,
    output_weight,
    gate_weight,
    up_weight,
    down_weight,
    input_gain,
    query_gain,
    key_gain,
    attn_gain,
    ffn_gain,
    ffn_out_gain,
    cotangent,
):
    span, width = tokens.shape
    head_dim = key_weight.shape[1]
    heads = query_weight.shape[1] // head_dim
    hq = heads * head_dim
    ff = gate_weight.shape[1]
    devices = lax.axis_size(ALL)
    hops = max(1, WINDOW // span)
    extent = hops * span + span
    scale = 1.0 / math.sqrt(head_dim)
    core = lax.axis_index("c")
    rows = query_weight.shape[0]
    columns = jnp.concatenate([gate_weight, up_weight], axis=1)
    columns = jnp.pad(columns, ((0, 8 - rows), (0, 0)))
    packed = jnp.concatenate([columns, output_weight, down_weight[:8], down_weight[8:]], axis=1)
    gathered = lax.all_gather(packed, ALL, axis=0, tiled=True)
    qkv = jnp.concatenate([query_weight, key_weight, value_weight], axis=1)
    qkv = lax.all_gather(jnp.pad(qkv, ((0, 8 - rows), (0, 0))), ("z", "c"), axis=0, tiled=False)
    qkv = qkv[:, :rows].reshape(8 * rows, -1)
    qkv = jnp.concatenate(
        [
            lax.dynamic_slice_in_dim(part, core * (part.shape[1] // 2), part.shape[1] // 2, 1)
            for part in (qkv[:, :hq], qkv[:, hq : hq + head_dim], qkv[:, hq + head_dim :])
        ],
        axis=1,
    )
    qkv = spread(jnp.broadcast_to(qkv, (16,) + qkv.shape), ("y", "x")).reshape(16 * 8 * rows, -1)
    other = swap_core(qkv)
    left = jnp.where(core == 0, qkv, other)
    right = jnp.where(core == 0, other, qkv)
    half, small = hq // 2, head_dim // 2
    full_query = jnp.concatenate([left[:, :half], right[:, :half]], axis=1)
    full_key = jnp.concatenate([left[:, half : half + small], right[:, half : half + small]], axis=1)
    full_value = jnp.concatenate([left[:, half + small :], right[:, half + small :]], axis=1)
    full_query, full_key, full_value = lax.optimization_barrier((full_query, full_key, full_value))

    place = jnp.arange(devices * 8, dtype=jnp.int32)
    pad_source = jnp.where(place % 8 < rows, place // 8 * rows + place % 8, -1)
    place = jnp.arange(width, dtype=jnp.int32)
    r, yx, c, z = place % rows, place // rows % 16, place // (rows * 16) % 2, place // (rows * 32)
    wide_source = ((yx * 4 + z) * 2 + c) * rows + r
    place = jnp.arange(2 * 16 * 24, dtype=jnp.int32)
    zr, x, y, c = place % 24, place // 24 % 4, place // (24 * 4) % 4, place // (24 * 16)
    c = jnp.where(core == 0, c, 1 - c)
    last_source = jnp.where(zr < 4 * rows, (((y * 4 + x) * 4 + zr // rows) * 2 + c) * rows + zr % rows, -1)

    group = lax.axis_index(ALL)
    group_ids = jnp.arange(starts.shape[0], dtype=jnp.int32)
    first_group = jnp.max(jnp.where((group_ids <= group) & (starts == 1), group_ids, 0))
    seq_first = first_group * span
    query_global = group * span + jnp.arange(span, dtype=jnp.int32)
    position = query_global - seq_first
    x_float = tokens.astype(jnp.float32)
    normed_in = rms_scale(x_float, input_gain).astype(bf16)
    query_pre = product(normed_in, full_query).reshape(span, heads, head_dim)
    key_pre = product(normed_in, full_key).reshape(span, 1, head_dim)
    value_bf = product(normed_in, full_value).astype(bf16)
    cosine, sine = rope_tables(position, head_dim)
    prepare = partial(head_prep, cosine=cosine, sine=sine)
    query_bf = prepare(query_pre, query_gain).astype(bf16)
    key_bf = prepare(key_pre, key_gain).astype(bf16).reshape(span, head_dim)
    pair = jnp.concatenate([key_bf, value_bf], axis=1)
    received = [shifted(pair, step) for step in range(hops, 0, -1)]
    both_all = jnp.concatenate(received + [pair], axis=0)
    keys_all = both_all[:, :head_dim]
    values_all = both_all[:, head_dim:]
    key_global = group * span - hops * span + jnp.arange(extent, dtype=jnp.int32)
    offset = query_global[:, None] - key_global[None, :]
    valid = (offset >= 0) & (offset < WINDOW) & (key_global[None, :] >= seq_first)
    query_flat = query_bf.reshape(span * heads, head_dim)
    scores = (transposed_right(query_flat, keys_all) * scale).reshape(span, heads, extent)
    scores = jnp.where(valid[:, None, :], scores, -1e30)
    peak = jnp.max(scores, axis=-1, keepdims=True)
    log_total = peak + jnp.log(jnp.sum(jnp.exp(scores - peak), axis=-1, keepdims=True))
    probs = jnp.exp(scores - log_total).reshape(span * heads, extent)
    probs_bf = probs.astype(bf16)
    attended_bf = product(probs_bf, values_all).reshape(span, heads * head_dim).astype(bf16)
    output, low_own, low_other, grads_wide, d_resid, d_attended_bf, ffn_gains = ffn(
        core.astype(jnp.int32).reshape(1), attended_bf, tokens, cotangent, gathered, attn_gain, ffn_gain, ffn_out_gain, pad_source, wide_source
    )
    wide = lax.psum_scatter(grads_wide, ("z", "c"), scatter_dimension=0, tiled=True)
    low_other = swap_core(low_other)
    bound = (seq_first - (group * span - hops * span)).reshape(1)
    cosine, sine = cosine[:, 0], sine[:, 0]
    d_own, d_near, d_far, d_query_pre_bf, grad_query_gain = attention_back(
        bound, query_bf.reshape(span, hq), both_all, d_attended_bf, query_pre.reshape(span, hq), cosine, sine, query_gain
    )
    d_near = shifted(d_near, -1)
    d_far = shifted(d_far, -2)
    part_low = (low_own.astype(f32) + low_other.astype(f32)).astype(bf16)
    d_query_pre_bf, part_low = lax.optimization_barrier((d_query_pre_bf, part_low))
    near_low = spread(part_low.reshape(16, 4 * 24, width), ("y", "x"))
    half_rows = last_source.shape[0] // 2
    grads_query, d_normed, turned = query_back(d_query_pre_bf, normed_in, last_source, full_query)
    other_query = swap_core(grads_query[half_rows:])
    grads_both, input_grad, gains = key_back(
        d_own, d_near, d_far, key_pre.reshape(span, head_dim), cosine, sine, key_gain, turned, full_key, full_value,
        d_normed, tokens, input_gain, d_resid, ffn_gains, grad_query_gain,
    )
    other_both = swap_core(grads_both[half_rows:])
    gains = gains.reshape(2, -1)
    part_qkv = jnp.concatenate(
        [
            (grads_query[:half_rows].astype(f32) + other_query.astype(f32)).astype(bf16),
            (grads_both[:half_rows].astype(f32) + other_both.astype(f32)).astype(bf16),
        ],
        axis=1,
    ).reshape(16, 24, -1)

    gains = gains + swap_core(gains)
    carried = jnp.concatenate(high_low(gains), axis=0)
    part_qkv = jnp.concatenate(
        [part_qkv[:, : 4 * rows], jnp.broadcast_to(carried, (16,) + carried.shape)], axis=1
    )
    part_qkv, near_low, wide = lax.optimization_barrier((part_qkv, near_low, wide))
    near_qkv = spread(part_qkv, ("y", "x"))
    low = jnp.sum(near_low.astype(f32), axis=0)
    wide = jnp.pad(wide.reshape(4, 4 * rows, 2 * ff), ((0, 0), (0, 24 - 4 * rows), (0, 0)))
    wide = ring_sum(wide, "y")[: 4 * rows].astype(bf16).reshape(4, rows, 2 * ff)
    near_qkv, wide = lax.optimization_barrier((near_qkv, wide))
    wide = ring_sum(jnp.pad(wide, ((0, 0), (0, 8 - rows), (0, 0))), "x")
    near_qkv = jnp.sum(near_qkv.astype(f32), axis=0)
    gains = (near_qkv[4 * rows : 4 * rows + 2] + near_qkv[4 * rows + 2 :]).reshape(4, -1)
    carried = jnp.concatenate(high_low(gains), axis=0)
    low = low.astype(bf16).reshape(4, 3, 8, width)
    low_columns = jnp.pad(near_qkv[: 4 * rows].astype(bf16).reshape(4, rows, -1), ((0, 0), (0, 8 - rows), (0, 0)))
    last = jnp.concatenate(
        [low_columns, low[:, 0], low[:, 1], low[:, 2], jnp.broadcast_to(carried, (4,) + carried.shape)],
        axis=2,
    )
    last = ring_sum(last, "z")
    sum_gate = wide[:rows, :ff]
    sum_up = wide[:rows, ff:]
    begin = hq + 2 * head_dim
    sum_qkv = last[:rows, :begin]
    sum_down = jnp.concatenate([last[:, begin : begin + width], last[:, begin + width : begin + 2 * width]], axis=0)
    sum_output = last[:, begin + 2 * width : begin + 3 * width]
    gains = last[:, begin + 3 * width :]
    gains = (gains[:4] + gains[4:]).reshape(-1)
    outs, begin = [], 0
    for size in (width, head_dim, head_dim, width, width, width):
        outs.append(gains[begin : begin + size])
        begin += size
    return (
        output,
        input_grad,
        sum_qkv[:, :hq],
        sum_qkv[:, hq : hq + head_dim],
        sum_qkv[:, hq + head_dim :],
        sum_output,
        sum_gate,
        sum_up,
        sum_down,
        *outs,
    )


def solution(mesh):
    inner = Mesh(mesh.devices.reshape(4, 4, 4, 2), ALL)
    split = P(ALL, None)
    return jax.shard_map(
        body,
        mesh=inner,
        in_specs=(split, P()) + (split,) * 7 + (P(),) * 6 + (split,),
        out_specs=(split,) * 9 + (P(),) * 6,
        check_vma=False,
    )
```

```python
from functools import partial
import math

import jax
import jax.numpy as jnp
from jax import lax
from jax.experimental import pallas as pl
from jax.experimental.pallas import tpu as pltpu
from jax.sharding import Mesh, PartitionSpec as P

WINDOW = 512
ALL = ("y", "x", "z", "c")

norm_epsilon = 1e-06
rope_base = 10000.0
GELU_A = math.sqrt(2.0 / math.pi)
GELU_B = 0.044715
bf16 = jnp.bfloat16
f32 = jnp.float32


def shifted(value, steps):
    count = lax.axis_size(ALL)
    leading, last = (max(0, -steps), min(count, count - steps))
    return lax.ppermute(value, ALL, [(source, source + steps) for source in range(leading, last)])


def rms_scale(values, gain):
    mean_square = jnp.mean(values * values, axis=-1, keepdims=True)
    return values * lax.rsqrt(mean_square + norm_epsilon) * gain


def rope_tables(position, head_dim):
    half = head_dim // 2
    exponent = jnp.arange(half, dtype=jnp.float32) * (2.0 / head_dim)
    inverse = jnp.power(jnp.float32(rope_base), -exponent)
    angles = position.astype(jnp.float32)[:, None] * inverse[None, :]
    return (jnp.cos(angles)[:, None, :], jnp.sin(angles)[:, None, :])


def head_prep(pre, gain, cosine, sine):
    normed = rms_scale(pre, gain)
    half = normed.shape[-1] // 2
    first = normed[..., :half]
    second = normed[..., half:]
    return jnp.concatenate(
        [first * cosine - second * sine, second * cosine + first * sine], axis=-1
    )


def gated(gate, upward):
    return jax.nn.gelu(gate, approximate=True) * upward


def product(left, right):
    return jnp.dot(left, right, preferred_element_type=jnp.float32)


def transposed_left(left, right):
    return lax.dot_general(
        left, right, (((0,), (0,)), ((), ())), preferred_element_type=jnp.float32
    )


def transposed_right(left, right):
    return lax.dot_general(
        left, right, (((1,), (1,)), ((), ())), preferred_element_type=jnp.float32
    )


def swap_core(value):
    return lax.ppermute(value, "c", [(0, 1), (1, 0)])


def halves(value, axis):
    core = lax.axis_index("c")
    mine = lax.dynamic_index_in_dim(value, core, axis, keepdims=False)
    theirs = lax.dynamic_index_in_dim(value, 1 - core, axis, keepdims=False)
    return mine, theirs


def core_sum(value, axis):
    mine, theirs = halves(value.astype(bf16), axis)
    return (mine.astype(f32) + swap_core(theirs).astype(f32)).astype(bf16)


def chosen(rows, source):
    return (jnp.arange(rows, dtype=jnp.int32)[:, None] == source[None, :]).astype(bf16)


def spread(value, axes):
    return lax.all_to_all(value, axes, split_axis=0, concat_axis=0, tiled=True)


def ring_sum(blocks, axis):
    place = lax.axis_index(axis)
    total = lax.dynamic_index_in_dim(blocks, place, 0, keepdims=False).astype(f32)
    for step in (1, 3, 2):
        block = lax.dynamic_index_in_dim(blocks, lax.rem(place + step, 4), 0, keepdims=False)
        total = total + lax.ppermute(block, axis, [(i, (i + step) % 4) for i in range(4)]).astype(f32)
    return total


def high_low(value):
    high = value.astype(bf16)
    low = (value - high.astype(f32)).astype(bf16)
    return high, low


def rms_inverse(values):
    return lax.rsqrt(jnp.mean(values * values, axis=-1, keepdims=True) + norm_epsilon)


def rms_back(values, inverse, gain, grad):
    scaled = grad * gain
    kept = values * inverse
    back = inverse * (scaled - kept * jnp.mean(scaled * kept, axis=-1, keepdims=True))
    return back, jnp.sum(grad * kept, axis=0, keepdims=True)


def one_hot(source, count):
    return (lax.broadcasted_iota(jnp.int32, (count, source.shape[1]), 0) == source).astype(f32).astype(bf16)


CHUNK = 1024


def ffn_kernel(
    core, attended, tokens, cotangent, gathered, attn_gain, ffn_gain, out_gain, pad_source, last_source,
    output, grad_own, grad_other, grad_wide, d_resid, d_attended, gains,
    grad_low, wide, low, first, second, mixed, normed_pad, normed_turned, projected, resid, pad_rows, d_down, down, d_pad, down_rows, sems,
):
    span, width = tokens.shape
    ff = mixed.shape[1]
    steps = ff // CHUNK
    copies = [pltpu.make_async_copy(gathered.at[:, 2 * ff :], low, sems.at[0])]
    for step in range(2 * steps):
        part = pl.ds((step // 2) * CHUNK + (step % 2) * ff, CHUNK)
        copies.append(pltpu.make_async_copy(gathered.at[:, part], wide.at[:, part], sems.at[1 + step]))
    for copy in copies:
        copy.start()
    pad_rows[...] = one_hot(pad_source[...], width)
    copies[0].wait()
    projected[...] = product(attended[...], low[:, :width])
    value = projected[...]
    resid[...] = tokens[...].astype(f32) + value * rms_inverse(value) * attn_gain[...]
    value = resid[...]
    normed = (value * rms_inverse(value) * ffn_gain[...]).astype(bf16)
    normed_pad[...] = product(normed, pad_rows[...]).astype(bf16)
    normed_turned[...] = product(normed, one_hot(last_source[...], width)).astype(bf16).T
    down[...] = jnp.zeros_like(down)

    for step in range(steps):
        block = pl.ds(step * (CHUNK // 2), CHUNK // 2)
        parts = [low[block, begin : begin + width].astype(f32).reshape(CHUNK // 16, 8, width) for begin in (width, 2 * width)]
        down_rows[step * CHUNK : (step + 1) * CHUNK, :] = (
            jnp.concatenate(parts, axis=1).reshape(CHUNK, width).astype(bf16)
        )

    for step in range(steps):
        here = pl.ds(step * CHUNK, CHUNK)
        there = pl.ds(ff + step * CHUNK, CHUNK)
        copies[1 + 2 * step].wait()
        copies[2 + 2 * step].wait()
        gate = product(normed_pad[...], wide[:, here])
        upward = product(normed_pad[...], wide[:, there])
        square = gate * gate
        bend = jnp.tanh(gate * (GELU_A + GELU_A * GELU_B * square))
        half = 0.5 + 0.5 * bend
        curve = gate * half
        slope = half + 0.5 * gate * (1.0 - bend * bend) * (GELU_A + 3.0 * GELU_A * GELU_B * square)
        first[:, here] = curve
        second[:, here] = slope * upward
        mixed[:, here] = (curve * upward).astype(bf16)
        down[...] += product(mixed[:, here], down_rows[here, :])

    value = down[...]
    inverse = rms_inverse(value)
    output[...] = (resid[...] + value * inverse * out_gain[...]).astype(bf16)
    back, gains[0:1, :] = rms_back(value, inverse, out_gain[...], cotangent[...].astype(f32))
    d_down[...] = back.astype(bf16)
    d_pad[...] = jnp.zeros_like(d_pad)
    for step in range(steps):
        here = pl.ds(step * CHUNK, CHUNK)
        there = pl.ds(ff + step * CHUNK, CHUNK)
        grad = transposed_left(mixed[:, here], d_down[...]).astype(bf16).reshape(CHUNK // 128, 4, 2, 16, width)
        blocks = pl.ds(step * (CHUNK // 128), CHUNK // 128)
        grad_low[0, blocks, :, :16] = grad[:, :, 0]
        grad_low[1, blocks, :, :16] = grad[:, :, 1]
        d_mixed = transposed_right(d_down[...], down_rows[here, :])
        d_gate = (d_mixed * second[:, here]).astype(bf16)
        d_upward = (d_mixed * first[:, here]).astype(bf16)
        grad_wide[:, here] = product(normed_turned[...], d_gate).astype(bf16)
        grad_wide[:, there] = product(normed_turned[...], d_upward).astype(bf16)
        d_pad[...] += transposed_right(d_gate, wide[:, here]) + transposed_right(d_upward, wide[:, there])
    out_copies = []
    for half, grad in enumerate((grad_own, grad_other)):
        source = grad_low.at[core[0] if half == 0 else 1 - core[0]]
        out_copies.append(pltpu.make_async_copy(source.at[:, :, :16], grad.at[:, :, :16], sems.at[half]))
        out_copies.append(pltpu.make_async_copy(source.at[:, :, 16:], grad.at[:, :, 16:], sems.at[2 + half]))
    out_copies[0].start()
    out_copies[2].start()
    high, lower = high_low(d_pad[...])
    d_normed = transposed_right(high, pad_rows[...]) + transposed_right(lower, pad_rows[...])
    value = resid[...]
    back, gains[1:2, :] = rms_back(value, rms_inverse(value), ffn_gain[...], d_normed)
    back = cotangent[...].astype(f32) + back
    d_resid[...] = back
    value = projected[...]
    back, gains[2:3, :] = rms_back(value, rms_inverse(value), attn_gain[...], back)
    back = back.astype(bf16)
    grad = transposed_left(attended[...], back).reshape(16, 4, 2, 8, width)
    grad_low[0, :, :, 16:] = grad[:, :, 0].astype(bf16)
    grad_low[1, :, :, 16:] = grad[:, :, 1].astype(bf16)
    out_copies[1].start()
    out_copies[3].start()
    d_attended[...] = transposed_right(back, low[:, :width]).astype(bf16)
    for copy in out_copies:
        copy.wait()


def ffn(core, attended, tokens, cotangent, gathered, attn_gain, ffn_gain, out_gain, pad_source, last_source):
    span, width = tokens.shape
    hq = attended.shape[1]
    ff = (gathered.shape[1] - 3 * width) // 2
    padded, spaced = gathered.shape[0], last_source.shape[0]
    vmem = pl.BlockSpec(memory_space=pltpu.VMEM)
    shape = jax.ShapeDtypeStruct
    return pl.pallas_call(
        ffn_kernel,
        out_shape=(
            shape((span, width), bf16),
            shape((16, 4, 24, width), bf16),
            shape((16, 4, 24, width), bf16),
            shape((spaced, 2 * ff), bf16),
            shape((span, width), f32),
            shape((span, hq), bf16),
            shape((3, width), f32),
        ),
        in_specs=[pl.BlockSpec(memory_space=pltpu.SMEM)] + [vmem] * 3 + [pl.BlockSpec(memory_space=pl.ANY)] + [vmem] * 5,
        out_specs=(vmem, pl.BlockSpec(memory_space=pl.ANY), pl.BlockSpec(memory_space=pl.ANY)) + (vmem,) * 4,
        scratch_shapes=[
            pltpu.VMEM((2, 16, 4, 24, width), bf16),
            pltpu.VMEM((padded, 2 * ff), bf16),
            pltpu.VMEM((padded, 3 * width), bf16),
            pltpu.VMEM((span, ff), f32),
            pltpu.VMEM((span, ff), f32),
            pltpu.VMEM((span, ff), bf16),
            pltpu.VMEM((span, padded), bf16),
            pltpu.VMEM((spaced, span), bf16),
            pltpu.VMEM((span, width), f32),
            pltpu.VMEM((span, width), f32),
            pltpu.VMEM((width, padded), bf16),
            pltpu.VMEM((span, width), bf16),
            pltpu.VMEM((span, width), f32),
            pltpu.VMEM((span, padded), f32),
            pltpu.VMEM((ff, width), bf16),
            pltpu.SemaphoreType.DMA((1 + 2 * (ff // CHUNK),)),
        ],
        compiler_params=pltpu.CompilerParams(vmem_limit_bytes=56 * 1024 * 1024),
        cost_estimate=pl.CostEstimate(flops=9 * 10**9, bytes_accessed=24 * 2**20, transcendentals=span * ff),
        name="ffn",
    )(
        core, attended, tokens, cotangent, gathered, attn_gain[None], ffn_gain[None], out_gain[None],
        pad_source[None], last_source[None],
    )


def turn_back(grad, cosine, sine):
    half = grad.shape[1] // 2
    first, second = grad[:, :half], grad[:, half:]
    return jnp.concatenate([first * cosine + second * sine, second * cosine - first * sine], axis=1)


def attention_back_kernel(
    bound, queries, both, d_attended, query_pre, cosine, sine, query_gain,
    d_own, d_near, d_far, d_query_pre, grad_gain, d_both,
):
    span, hq = queries.shape
    extent = both.shape[0]
    head_dim = both.shape[1] // 2
    scale = 1.0 / math.sqrt(head_dim)
    offset = (
        lax.broadcasted_iota(jnp.int32, (span, extent), 0)
        - lax.broadcasted_iota(jnp.int32, (span, extent), 1)
        + (extent - span)
    )
    place = lax.broadcasted_iota(jnp.int32, (span, extent), 1)
    valid = (offset >= 0) & (offset < WINDOW) & (place >= bound[0])
    keys, values = both[:, :head_dim], both[:, head_dim:]
    gain_sum = jnp.zeros((1, head_dim), f32)
    for head in range(hq // head_dim):
        here = pl.ds(head * head_dim, head_dim)
        query, d_att = queries[:, here], d_attended[:, here]
        scores = jnp.where(valid, transposed_right(query, keys) * scale, -1e30)
        weights = jnp.exp(scores - jnp.max(scores, axis=-1, keepdims=True))
        probs = weights * (1.0 / jnp.sum(weights, axis=-1, keepdims=True))
        d_probs = transposed_right(d_att, values)
        balance = jnp.sum(d_probs * probs, axis=-1, keepdims=True)
        d_scores = (probs * (d_probs - balance)).astype(bf16)
        d_query = (product(d_scores, keys) * scale).astype(bf16).astype(f32)
        d_key = transposed_left(d_scores, query) * scale
        d_value = transposed_left(probs.astype(bf16), d_att)
        if head == 0:
            d_both[:, :head_dim] = d_key
            d_both[:, head_dim:] = d_value
        else:
            d_both[:, :head_dim] += d_key
            d_both[:, head_dim:] += d_value
        pre = query_pre[:, here]
        back, gain_part = rms_back(pre, rms_inverse(pre), query_gain[...], turn_back(d_query, cosine[...], sine[...]))
        gain_sum += gain_part
        d_query_pre[:, here] = back.astype(bf16)
    grad_gain[...] = gain_sum
    d_far[...] = d_both[:span, :].astype(bf16)
    d_near[...] = d_both[span : 2 * span, :].astype(bf16)
    d_own[...] = d_both[2 * span :, :]


def attention_back(bound, queries, both, d_attended, query_pre, cosine, sine, query_gain):
    span, hq = queries.shape
    extent, pair = both.shape
    vmem = pl.BlockSpec(memory_space=pltpu.VMEM)
    shape = jax.ShapeDtypeStruct
    return pl.pallas_call(
        attention_back_kernel,
        out_shape=(
            shape((span, pair), f32),
            shape((span, pair), bf16),
            shape((span, pair), bf16),
            shape((span, hq), bf16),
            shape((1, pair // 2), f32),
        ),
        in_specs=[pl.BlockSpec(memory_space=pltpu.SMEM)] + [vmem] * 7,
        out_specs=(vmem,) * 5,
        scratch_shapes=[pltpu.VMEM((extent, pair), f32)],
        compiler_params=pltpu.CompilerParams(vmem_limit_bytes=48 * 1024 * 1024),
        cost_estimate=pl.CostEstimate(flops=12 * span * extent * hq, bytes_accessed=6 * 2**20, transcendentals=4 * span * extent),
        name="attention_back",
    )(bound, queries, both, d_attended, query_pre, cosine, sine, query_gain[None])


def query_back_kernel(d_query_pre, normed, source, weight, grads, d_normed, turned):
    turned[...] = product(normed[...], one_hot(source[...], normed.shape[1])).astype(bf16).T
    grads[...] = product(turned[...], d_query_pre[...]).astype(bf16)
    d_normed[...] = transposed_right(d_query_pre[...], weight[...])


def query_back(d_query_pre, normed, source, weight):
    span, width = normed.shape
    vmem = pl.BlockSpec(memory_space=pltpu.VMEM)
    shape = jax.ShapeDtypeStruct
    return pl.pallas_call(
        query_back_kernel,
        out_shape=(
            shape((source.shape[0], d_query_pre.shape[1]), bf16),
            shape((span, width), f32),
            shape((source.shape[0], span), bf16),
        ),
        in_specs=[vmem] * 4,
        out_specs=(vmem,) * 3,
        compiler_params=pltpu.CompilerParams(vmem_limit_bytes=48 * 1024 * 1024),
        cost_estimate=pl.CostEstimate(flops=10**9, bytes_accessed=4 * 2**20, transcendentals=0),
        name="query_back",
    )(d_query_pre, normed, source[None], weight)


def key_back_kernel(
    d_own, d_near, d_far, key_pre, cosine, sine, key_gain, turned, key_weight, value_weight, d_normed, tokens, input_gain,
    d_resid, ffn_gains, query_gain_grad, grads, input_grad, gains,
):
    head_dim = key_pre.shape[1]
    width = tokens.shape[1]
    total = d_own[...] + d_near[...].astype(f32) + d_far[...].astype(f32)
    d_key = total[:, :head_dim].astype(bf16).astype(f32)
    d_value = total[:, head_dim:].astype(bf16)
    pre = key_pre[...]
    back, gain_part = rms_back(pre, rms_inverse(pre), key_gain[...], turn_back(d_key, cosine[...], sine[...]))
    back = back.astype(bf16)
    grads[:, :head_dim] = product(turned[...], back).astype(bf16)
    grads[:, head_dim:] = product(turned[...], d_value).astype(bf16)
    d_in = d_normed[...] + transposed_right(back, key_weight[...]) + transposed_right(d_value, value_weight[...])
    value = tokens[...].astype(f32)
    back, gain_in = rms_back(value, rms_inverse(value), input_gain[...], d_in)
    input_grad[...] = (d_resid[...] + back).astype(bf16)
    parts = [gain_in, query_gain_grad[...], gain_part] + [ffn_gains[row : row + 1, :] for row in (2, 1, 0)]
    full = jnp.concatenate(parts, axis=1)
    half = full.shape[1] // 2
    gains[0:1, :] = full[:, :half]
    gains[1:2, :] = full[:, half:]


def key_back(
    d_own, d_near, d_far, key_pre, cosine, sine, key_gain, turned, key_weight, value_weight, d_normed, tokens, input_gain,
    d_resid, ffn_gains, query_gain_grad,
):
    span, width = tokens.shape
    head_dim = key_pre.shape[1]
    vmem = pl.BlockSpec(memory_space=pltpu.VMEM)
    shape = jax.ShapeDtypeStruct
    return pl.pallas_call(
        key_back_kernel,
        out_shape=(
            shape((turned.shape[0], 2 * head_dim), bf16),
            shape((span, width), bf16),
            shape((2, 2 * width + head_dim), f32),
        ),
        in_specs=[vmem] * 16,
        out_specs=(vmem,) * 3,
        compiler_params=pltpu.CompilerParams(vmem_limit_bytes=48 * 1024 * 1024),
        cost_estimate=pl.CostEstimate(flops=10**9, bytes_accessed=6 * 2**20, transcendentals=0),
        name="key_back",
    )(
        d_own, d_near, d_far, key_pre, cosine, sine, key_gain[None], turned, key_weight, value_weight, d_normed, tokens,
        input_gain[None], d_resid, ffn_gains, query_gain_grad,
    )


def body(
    tokens,
    starts,
    query_weight,
    key_weight,
    value_weight,
    output_weight,
    gate_weight,
    up_weight,
    down_weight,
    input_gain,
    query_gain,
    key_gain,
    attn_gain,
    ffn_gain,
    ffn_out_gain,
    cotangent,
):
    span, width = tokens.shape
    head_dim = key_weight.shape[1]
    heads = query_weight.shape[1] // head_dim
    hq = heads * head_dim
    ff = gate_weight.shape[1]
    devices = lax.axis_size(ALL)
    hops = max(1, WINDOW // span)
    extent = hops * span + span
    scale = 1.0 / math.sqrt(head_dim)
    core = lax.axis_index("c")
    rows = query_weight.shape[0]
    columns = jnp.concatenate([gate_weight, up_weight], axis=1)
    columns = jnp.pad(columns, ((0, 8 - rows), (0, 0)))
    packed = jnp.concatenate([columns, output_weight, down_weight[:8], down_weight[8:]], axis=1)
    gathered = lax.all_gather(packed, ALL, axis=0, tiled=True)
    qkv = jnp.concatenate([query_weight, key_weight, value_weight], axis=1)
    qkv = lax.all_gather(jnp.pad(qkv, ((0, 8 - rows), (0, 0))), ("z", "c"), axis=0, tiled=False)
    qkv = qkv[:, :rows].reshape(8 * rows, -1)
    qkv = jnp.concatenate(
        [
            lax.dynamic_slice_in_dim(part, core * (part.shape[1] // 2), part.shape[1] // 2, 1)
            for part in (qkv[:, :hq], qkv[:, hq : hq + head_dim], qkv[:, hq + head_dim :])
        ],
        axis=1,
    )
    qkv = spread(jnp.broadcast_to(qkv, (16,) + qkv.shape), ("y", "x")).reshape(16 * 8 * rows, -1)
    other = swap_core(qkv)
    left = jnp.where(core == 0, qkv, other)
    right = jnp.where(core == 0, other, qkv)
    half, small = hq // 2, head_dim // 2
    full_query = jnp.concatenate([left[:, :half], right[:, :half]], axis=1)
    full_key = jnp.concatenate([left[:, half : half + small], right[:, half : half + small]], axis=1)
    full_value = jnp.concatenate([left[:, half + small :], right[:, half + small :]], axis=1)
    full_query, full_key, full_value = lax.optimization_barrier((full_query, full_key, full_value))

    place = jnp.arange(devices * 8, dtype=jnp.int32)
    pad_source = jnp.where(place % 8 < rows, place // 8 * rows + place % 8, -1)
    place = jnp.arange(width, dtype=jnp.int32)
    r, yx, c, z = place % rows, place // rows % 16, place // (rows * 16) % 2, place // (rows * 32)
    wide_source = ((yx * 4 + z) * 2 + c) * rows + r
    place = jnp.arange(2 * 16 * 24, dtype=jnp.int32)
    zr, x, y, c = place % 24, place // 24 % 4, place // (24 * 4) % 4, place // (24 * 16)
    c = jnp.where(core == 0, c, 1 - c)
    last_source = jnp.where(zr < 4 * rows, (((y * 4 + x) * 4 + zr // rows) * 2 + c) * rows + zr % rows, -1)

    group = lax.axis_index(ALL)
    group_ids = jnp.arange(starts.shape[0], dtype=jnp.int32)
    first_group = jnp.max(jnp.where((group_ids <= group) & (starts == 1), group_ids, 0))
    seq_first = first_group * span
    query_global = group * span + jnp.arange(span, dtype=jnp.int32)
    position = query_global - seq_first
    x_float = tokens.astype(jnp.float32)
    normed_in = rms_scale(x_float, input_gain).astype(bf16)
    query_pre = product(normed_in, full_query).reshape(span, heads, head_dim)
    key_pre = product(normed_in, full_key).reshape(span, 1, head_dim)
    value_bf = product(normed_in, full_value).astype(bf16)
    cosine, sine = rope_tables(position, head_dim)
    prepare = partial(head_prep, cosine=cosine, sine=sine)
    query_bf = prepare(query_pre, query_gain).astype(bf16)
    key_bf = prepare(key_pre, key_gain).astype(bf16).reshape(span, head_dim)
    pair = jnp.concatenate([key_bf, value_bf], axis=1)
    received = [shifted(pair, step) for step in range(hops, 0, -1)]
    both_all = jnp.concatenate(received + [pair], axis=0)
    keys_all = both_all[:, :head_dim]
    values_all = both_all[:, head_dim:]
    key_global = group * span - hops * span + jnp.arange(extent, dtype=jnp.int32)
    offset = query_global[:, None] - key_global[None, :]
    valid = (offset >= 0) & (offset < WINDOW) & (key_global[None, :] >= seq_first)
    query_flat = query_bf.reshape(span * heads, head_dim)
    scores = (transposed_right(query_flat, keys_all) * scale).reshape(span, heads, extent)
    scores = jnp.where(valid[:, None, :], scores, -1e30)
    peak = jnp.max(scores, axis=-1, keepdims=True)
    log_total = peak + jnp.log(jnp.sum(jnp.exp(scores - peak), axis=-1, keepdims=True))
    probs = jnp.exp(scores - log_total).reshape(span * heads, extent)
    probs_bf = probs.astype(bf16)
    attended_bf = product(probs_bf, values_all).reshape(span, heads * head_dim).astype(bf16)
    output, low_own, low_other, grads_wide, d_resid, d_attended_bf, ffn_gains = ffn(
        core.astype(jnp.int32).reshape(1), attended_bf, tokens, cotangent, gathered, attn_gain, ffn_gain, ffn_out_gain, pad_source, wide_source
    )
    wide = lax.psum_scatter(grads_wide, ("z", "c"), scatter_dimension=0, tiled=True)
    low_other = swap_core(low_other)
    bound = (seq_first - (group * span - hops * span)).reshape(1)
    cosine, sine = cosine[:, 0], sine[:, 0]
    d_own, d_near, d_far, d_query_pre_bf, grad_query_gain = attention_back(
        bound, query_bf.reshape(span, hq), both_all, d_attended_bf, query_pre.reshape(span, hq), cosine, sine, query_gain
    )
    d_near = shifted(d_near, -1)
    d_far = shifted(d_far, -2)
    part_low = (low_own.astype(f32) + low_other.astype(f32)).astype(bf16)
    d_query_pre_bf, part_low = lax.optimization_barrier((d_query_pre_bf, part_low))
    near_low = spread(part_low.reshape(16, 4 * 24, width), ("y", "x"))
    half_rows = last_source.shape[0] // 2
    grads_query, d_normed, turned = query_back(d_query_pre_bf, normed_in, last_source, full_query)
    other_query = swap_core(grads_query[half_rows:])
    grads_both, input_grad, gains = key_back(
        d_own, d_near, d_far, key_pre.reshape(span, head_dim), cosine, sine, key_gain, turned, full_key, full_value,
        d_normed, tokens, input_gain, d_resid, ffn_gains, grad_query_gain,
    )
    other_both = swap_core(grads_both[half_rows:])
    part_qkv = jnp.concatenate(
        [
            (grads_query[:half_rows].astype(f32) + other_query.astype(f32)).astype(bf16),
            (grads_both[:half_rows].astype(f32) + other_both.astype(f32)).astype(bf16),
        ],
        axis=1,
    ).reshape(16, 24, -1)

    gains = gains + swap_core(gains)
    carried = jnp.concatenate(high_low(gains), axis=0)
    part_qkv = jnp.concatenate(
        [part_qkv[:, : 4 * rows], jnp.broadcast_to(carried, (16,) + carried.shape)], axis=1
    )
    part_qkv, near_low, wide = lax.optimization_barrier((part_qkv, near_low, wide))
    near_qkv = spread(part_qkv, ("y", "x"))
    low = jnp.sum(near_low.astype(f32), axis=0)
    wide = jnp.pad(wide.reshape(4, 4 * rows, 2 * ff), ((0, 0), (0, 24 - 4 * rows), (0, 0)))
    wide = ring_sum(wide, "y")[: 4 * rows].astype(bf16).reshape(4, rows, 2 * ff)
    near_qkv, wide = lax.optimization_barrier((near_qkv, wide))
    wide = ring_sum(jnp.pad(wide, ((0, 0), (0, 8 - rows), (0, 0))), "x")
    near_qkv = jnp.sum(near_qkv.astype(f32), axis=0)
    gains = (near_qkv[4 * rows : 4 * rows + 2] + near_qkv[4 * rows + 2 :]).reshape(4, -1)
    carried = jnp.concatenate(high_low(gains), axis=0)
    low = low.astype(bf16).reshape(4, 3, 8, width)
    low_columns = jnp.pad(near_qkv[: 4 * rows].astype(bf16).reshape(4, rows, -1), ((0, 0), (0, 8 - rows), (0, 0)))
    last = jnp.concatenate(
        [low_columns, low[:, 0], low[:, 1], low[:, 2], jnp.broadcast_to(carried, (4,) + carried.shape)],
        axis=2,
    )
    last = ring_sum(last, "z")
    sum_gate = wide[:rows, :ff]
    sum_up = wide[:rows, ff:]
    begin = hq + 2 * head_dim
    sum_qkv = last[:rows, :begin]
    sum_down = jnp.concatenate([last[:, begin : begin + width], last[:, begin + width : begin + 2 * width]], axis=0)
    sum_output = last[:, begin + 2 * width : begin + 3 * width]
    gains = last[:, begin + 3 * width :]
    gains = (gains[:4] + gains[4:]).reshape(-1)
    outs, begin = [], 0
    for size in (width, head_dim, head_dim, width, width, width):
        outs.append(gains[begin : begin + size])
        begin += size
    return (
        output,
        input_grad,
        sum_qkv[:, :hq],
        sum_qkv[:, hq : hq + head_dim],
        sum_qkv[:, hq + head_dim :],
        sum_output,
        sum_gate,
        sum_up,
        sum_down,
        *outs,
    )


def solution(mesh):
    inner = Mesh(mesh.devices.reshape(4, 4, 4, 2), ALL)
    split = P(ALL, None)
    return jax.shard_map(
        body,
        mesh=inner,
        in_specs=(split, P()) + (split,) * 7 + (P(),) * 6 + (split,),
        out_specs=(split,) * 9 + (P(),) * 6,
        check_vma=False,
    )
```

```python
from functools import partial
import math

import jax
import jax.numpy as jnp
from jax import lax
from jax.experimental import pallas as pl
from jax.experimental.pallas import tpu as pltpu
from jax.sharding import Mesh, PartitionSpec as P

WINDOW = 512
ALL = ("y", "x", "z", "c")

norm_epsilon = 1e-06
rope_base = 10000.0
GELU_A = math.sqrt(2.0 / math.pi)
GELU_B = 0.044715
bf16 = jnp.bfloat16
f32 = jnp.float32


def shifted(value, steps):
    count = lax.axis_size(ALL)
    leading, last = (max(0, -steps), min(count, count - steps))
    return lax.ppermute(value, ALL, [(source, source + steps) for source in range(leading, last)])


def rms_scale(values, gain):
    mean_square = jnp.mean(values * values, axis=-1, keepdims=True)
    return values * lax.rsqrt(mean_square + norm_epsilon) * gain


def rope_tables(position, head_dim):
    half = head_dim // 2
    exponent = jnp.arange(half, dtype=jnp.float32) * (2.0 / head_dim)
    inverse = jnp.power(jnp.float32(rope_base), -exponent)
    angles = position.astype(jnp.float32)[:, None] * inverse[None, :]
    return (jnp.cos(angles)[:, None, :], jnp.sin(angles)[:, None, :])


def head_prep(pre, gain, cosine, sine):
    normed = rms_scale(pre, gain)
    half = normed.shape[-1] // 2
    first = normed[..., :half]
    second = normed[..., half:]
    return jnp.concatenate(
        [first * cosine - second * sine, second * cosine + first * sine], axis=-1
    )


def gated(gate, upward):
    return jax.nn.gelu(gate, approximate=True) * upward


def product(left, right):
    return jnp.dot(left, right, preferred_element_type=jnp.float32)


def transposed_left(left, right):
    return lax.dot_general(
        left, right, (((0,), (0,)), ((), ())), preferred_element_type=jnp.float32
    )


def transposed_right(left, right):
    return lax.dot_general(
        left, right, (((1,), (1,)), ((), ())), preferred_element_type=jnp.float32
    )


def swap_core(value):
    return lax.ppermute(value, "c", [(0, 1), (1, 0)])


def halves(value, axis):
    core = lax.axis_index("c")
    mine = lax.dynamic_index_in_dim(value, core, axis, keepdims=False)
    theirs = lax.dynamic_index_in_dim(value, 1 - core, axis, keepdims=False)
    return mine, theirs


def core_sum(value, axis):
    mine, theirs = halves(value.astype(bf16), axis)
    return (mine.astype(f32) + swap_core(theirs).astype(f32)).astype(bf16)


def chosen(rows, source):
    return (jnp.arange(rows, dtype=jnp.int32)[:, None] == source[None, :]).astype(bf16)


def spread(value, axes):
    return lax.all_to_all(value, axes, split_axis=0, concat_axis=0, tiled=True)


def ring_sum(blocks, axis):
    place = lax.axis_index(axis)
    total = lax.dynamic_index_in_dim(blocks, place, 0, keepdims=False).astype(f32)
    for step in (1, 3, 2):
        block = lax.dynamic_index_in_dim(blocks, lax.rem(place + step, 4), 0, keepdims=False)
        total = total + lax.ppermute(block, axis, [(i, (i + step) % 4) for i in range(4)]).astype(f32)
    return total


def high_low(value):
    high = value.astype(bf16)
    low = (value - high.astype(f32)).astype(bf16)
    return high, low


def rms_inverse(values):
    return lax.rsqrt(jnp.mean(values * values, axis=-1, keepdims=True) + norm_epsilon)


def rms_back(values, inverse, gain, grad):
    scaled = grad * gain
    kept = values * inverse
    back = inverse * (scaled - kept * jnp.mean(scaled * kept, axis=-1, keepdims=True))
    return back, jnp.sum(grad * kept, axis=0, keepdims=True)


def one_hot(source, count):
    return (lax.broadcasted_iota(jnp.int32, (count, source.shape[1]), 0) == source).astype(f32).astype(bf16)


CHUNK = 1024


def ffn_kernel(
    core, attended, tokens, cotangent, gathered, attn_gain, ffn_gain, out_gain, pad_source, last_source,
    output, grad_own, grad_other, grad_wide, d_resid, d_attended, gains,
    grad_low, wide, low, first, second, mixed, normed_pad, normed_turned, projected, resid, pad_rows, d_down, down, d_pad, down_rows, sems,
):
    span, width = tokens.shape
    ff = mixed.shape[1]
    steps = ff // CHUNK
    copies = [pltpu.make_async_copy(gathered.at[:, 2 * ff :], low, sems.at[0])]
    for step in range(2 * steps):
        part = pl.ds((step // 2) * CHUNK + (step % 2) * ff, CHUNK)
        copies.append(pltpu.make_async_copy(gathered.at[:, part], wide.at[:, part], sems.at[1 + step]))
    for copy in copies:
        copy.start()
    pad_rows[...] = one_hot(pad_source[...], width)
    copies[0].wait()
    projected[...] = product(attended[...], low[:, :width])
    value = projected[...]
    resid[...] = tokens[...].astype(f32) + value * rms_inverse(value) * attn_gain[...]
    value = resid[...]
    normed = (value * rms_inverse(value) * ffn_gain[...]).astype(bf16)
    normed_pad[...] = product(normed, pad_rows[...]).astype(bf16)
    normed_turned[...] = product(normed, one_hot(last_source[...], width)).astype(bf16).T
    down[...] = jnp.zeros_like(down)

    for step in range(steps):
        block = pl.ds(step * (CHUNK // 2), CHUNK // 2)
        parts = [low[block, begin : begin + width].astype(f32).reshape(CHUNK // 16, 8, width) for begin in (width, 2 * width)]
        down_rows[step * CHUNK : (step + 1) * CHUNK, :] = (
            jnp.concatenate(parts, axis=1).reshape(CHUNK, width).astype(bf16)
        )

    for step in range(steps):
        here = pl.ds(step * CHUNK, CHUNK)
        there = pl.ds(ff + step * CHUNK, CHUNK)
        copies[1 + 2 * step].wait()
        copies[2 + 2 * step].wait()
        gate = product(normed_pad[...], wide[:, here])
        upward = product(normed_pad[...], wide[:, there])
        square = gate * gate
        bend = jnp.tanh(gate * (GELU_A + GELU_A * GELU_B * square))
        half = 0.5 + 0.5 * bend
        curve = gate * half
        slope = half + 0.5 * gate * (1.0 - bend * bend) * (GELU_A + 3.0 * GELU_A * GELU_B * square)
        first[:, here] = curve
        second[:, here] = slope * upward
        mixed[:, here] = (curve * upward).astype(bf16)
        down[...] += product(mixed[:, here], down_rows[here, :])

    value = down[...]
    inverse = rms_inverse(value)
    output[...] = (resid[...] + value * inverse * out_gain[...]).astype(bf16)
    back, gains[0:1, :] = rms_back(value, inverse, out_gain[...], cotangent[...].astype(f32))
    d_down[...] = back.astype(bf16)
    d_pad[...] = jnp.zeros_like(d_pad)
    for step in range(steps):
        here = pl.ds(step * CHUNK, CHUNK)
        there = pl.ds(ff + step * CHUNK, CHUNK)
        grad = transposed_left(mixed[:, here], d_down[...]).astype(bf16).reshape(CHUNK // 128, 4, 2, 16, width)
        blocks = pl.ds(step * (CHUNK // 128), CHUNK // 128)
        grad_low[0, blocks, :, :16] = grad[:, :, 0]
        grad_low[1, blocks, :, :16] = grad[:, :, 1]
        d_mixed = transposed_right(d_down[...], down_rows[here, :])
        d_gate = (d_mixed * second[:, here]).astype(bf16)
        d_upward = (d_mixed * first[:, here]).astype(bf16)
        grad_wide[:, here] = product(normed_turned[...], d_gate).astype(bf16)
        grad_wide[:, there] = product(normed_turned[...], d_upward).astype(bf16)
        d_pad[...] += transposed_right(d_gate, wide[:, here]) + transposed_right(d_upward, wide[:, there])
    out_copies = []
    for half, grad in enumerate((grad_own, grad_other)):
        source = grad_low.at[core[0] if half == 0 else 1 - core[0]]
        out_copies.append(pltpu.make_async_copy(source.at[:, :, :16], grad.at[:, :, :16], sems.at[half]))
        out_copies.append(pltpu.make_async_copy(source.at[:, :, 16:], grad.at[:, :, 16:], sems.at[2 + half]))
    out_copies[0].start()
    out_copies[2].start()
    high, lower = high_low(d_pad[...])
    d_normed = transposed_right(high, pad_rows[...]) + transposed_right(lower, pad_rows[...])
    value = resid[...]
    back, gains[1:2, :] = rms_back(value, rms_inverse(value), ffn_gain[...], d_normed)
    back = cotangent[...].astype(f32) + back
    d_resid[...] = back
    value = projected[...]
    back, gains[2:3, :] = rms_back(value, rms_inverse(value), attn_gain[...], back)
    back = back.astype(bf16)
    grad = transposed_left(attended[...], back).reshape(16, 4, 2, 8, width)
    grad_low[0, :, :, 16:] = grad[:, :, 0].astype(bf16)
    grad_low[1, :, :, 16:] = grad[:, :, 1].astype(bf16)
    out_copies[1].start()
    out_copies[3].start()
    d_attended[...] = transposed_right(back, low[:, :width]).astype(bf16)
    for copy in out_copies:
        copy.wait()


def ffn(core, attended, tokens, cotangent, gathered, attn_gain, ffn_gain, out_gain, pad_source, last_source):
    span, width = tokens.shape
    hq = attended.shape[1]
    ff = (gathered.shape[1] - 3 * width) // 2
    padded, spaced = gathered.shape[0], last_source.shape[0]
    vmem = pl.BlockSpec(memory_space=pltpu.VMEM)
    shape = jax.ShapeDtypeStruct
    return pl.pallas_call(
        ffn_kernel,
        out_shape=(
            shape((span, width), bf16),
            shape((16, 4, 24, width), bf16),
            shape((16, 4, 24, width), bf16),
            shape((spaced, 2 * ff), bf16),
            shape((span, width), f32),
            shape((span, hq), bf16),
            shape((3, width), f32),
        ),
        in_specs=[pl.BlockSpec(memory_space=pltpu.SMEM)] + [vmem] * 3 + [pl.BlockSpec(memory_space=pl.ANY)] + [vmem] * 5,
        out_specs=(vmem, pl.BlockSpec(memory_space=pl.ANY), pl.BlockSpec(memory_space=pl.ANY)) + (vmem,) * 4,
        scratch_shapes=[
            pltpu.VMEM((2, 16, 4, 24, width), bf16),
            pltpu.VMEM((padded, 2 * ff), bf16),
            pltpu.VMEM((padded, 3 * width), bf16),
            pltpu.VMEM((span, ff), f32),
            pltpu.VMEM((span, ff), f32),
            pltpu.VMEM((span, ff), bf16),
            pltpu.VMEM((span, padded), bf16),
            pltpu.VMEM((spaced, span), bf16),
            pltpu.VMEM((span, width), f32),
            pltpu.VMEM((span, width), f32),
            pltpu.VMEM((width, padded), bf16),
            pltpu.VMEM((span, width), bf16),
            pltpu.VMEM((span, width), f32),
            pltpu.VMEM((span, padded), f32),
            pltpu.VMEM((ff, width), bf16),
            pltpu.SemaphoreType.DMA((1 + 2 * (ff // CHUNK),)),
        ],
        compiler_params=pltpu.CompilerParams(vmem_limit_bytes=56 * 1024 * 1024),
        cost_estimate=pl.CostEstimate(flops=9 * 10**9, bytes_accessed=24 * 2**20, transcendentals=span * ff),
        name="ffn",
    )(
        core, attended, tokens, cotangent, gathered, attn_gain[None], ffn_gain[None], out_gain[None],
        pad_source[None], last_source[None],
    )


def turn_back(grad, cosine, sine):
    half = grad.shape[1] // 2
    first, second = grad[:, :half], grad[:, half:]
    return jnp.concatenate([first * cosine + second * sine, second * cosine - first * sine], axis=1)


def attention_back_kernel(
    bound, queries, both, d_attended, query_pre, cosine, sine, query_gain,
    d_own, d_near, d_far, d_query_pre, grad_gain, d_both,
):
    span, hq = queries.shape
    extent = both.shape[0]
    head_dim = both.shape[1] // 2
    scale = 1.0 / math.sqrt(head_dim)
    offset = (
        lax.broadcasted_iota(jnp.int32, (span, extent), 0)
        - lax.broadcasted_iota(jnp.int32, (span, extent), 1)
        + (extent - span)
    )
    place = lax.broadcasted_iota(jnp.int32, (span, extent), 1)
    valid = (offset >= 0) & (offset < WINDOW) & (place >= bound[0])
    keys, values = both[:, :head_dim], both[:, head_dim:]
    gain_sum = jnp.zeros((1, head_dim), f32)
    for head in range(hq // head_dim):
        here = pl.ds(head * head_dim, head_dim)
        query, d_att = queries[:, here], d_attended[:, here]
        scores = jnp.where(valid, transposed_right(query, keys) * scale, -1e30)
        weights = jnp.exp(scores - jnp.max(scores, axis=-1, keepdims=True))
        probs = weights * (1.0 / jnp.sum(weights, axis=-1, keepdims=True))
        d_probs = transposed_right(d_att, values)
        balance = jnp.sum(d_probs * probs, axis=-1, keepdims=True)
        d_scores = (probs * (d_probs - balance)).astype(bf16)
        d_query = (product(d_scores, keys) * scale).astype(bf16).astype(f32)
        d_key = transposed_left(d_scores, query) * scale
        d_value = transposed_left(probs.astype(bf16), d_att)
        if head == 0:
            d_both[:, :head_dim] = d_key
            d_both[:, head_dim:] = d_value
        else:
            d_both[:, :head_dim] += d_key
            d_both[:, head_dim:] += d_value
        pre = query_pre[:, here]
        back, gain_part = rms_back(pre, rms_inverse(pre), query_gain[...], turn_back(d_query, cosine[...], sine[...]))
        gain_sum += gain_part
        d_query_pre[:, here] = back.astype(bf16)
    grad_gain[...] = gain_sum
    d_far[...] = d_both[:span, :].astype(bf16)
    d_near[...] = d_both[span : 2 * span, :].astype(bf16)
    d_own[...] = d_both[2 * span :, :]


def attention_back(bound, queries, both, d_attended, query_pre, cosine, sine, query_gain):
    span, hq = queries.shape
    extent, pair = both.shape
    vmem = pl.BlockSpec(memory_space=pltpu.VMEM)
    shape = jax.ShapeDtypeStruct
    return pl.pallas_call(
        attention_back_kernel,
        out_shape=(
            shape((span, pair), f32),
            shape((span, pair), bf16),
            shape((span, pair), bf16),
            shape((span, hq), bf16),
            shape((1, pair // 2), f32),
        ),
        in_specs=[pl.BlockSpec(memory_space=pltpu.SMEM)] + [vmem] * 7,
        out_specs=(vmem,) * 5,
        scratch_shapes=[pltpu.VMEM((extent, pair), f32)],
        compiler_params=pltpu.CompilerParams(vmem_limit_bytes=48 * 1024 * 1024),
        cost_estimate=pl.CostEstimate(flops=12 * span * extent * hq, bytes_accessed=6 * 2**20, transcendentals=4 * span * extent),
        name="attention_back",
    )(bound, queries, both, d_attended, query_pre, cosine, sine, query_gain[None])


def query_back_kernel(d_query_pre, normed, source, weight, grads, d_normed, turned):
    turned[...] = product(normed[...], one_hot(source[...], normed.shape[1])).astype(bf16).T
    grads[...] = product(turned[...], d_query_pre[...]).astype(bf16)
    d_normed[...] = transposed_right(d_query_pre[...], weight[...])


def query_back(d_query_pre, normed, source, weight):
    span, width = normed.shape
    vmem = pl.BlockSpec(memory_space=pltpu.VMEM)
    shape = jax.ShapeDtypeStruct
    return pl.pallas_call(
        query_back_kernel,
        out_shape=(
            shape((source.shape[0], d_query_pre.shape[1]), bf16),
            shape((span, width), f32),
            shape((source.shape[0], span), bf16),
        ),
        in_specs=[vmem] * 4,
        out_specs=(vmem,) * 3,
        compiler_params=pltpu.CompilerParams(vmem_limit_bytes=48 * 1024 * 1024),
        cost_estimate=pl.CostEstimate(flops=10**9, bytes_accessed=4 * 2**20, transcendentals=0),
        name="query_back",
    )(d_query_pre, normed, source[None], weight)


def key_back_kernel(
    d_own, d_near, d_far, key_pre, cosine, sine, key_gain, turned, key_weight, value_weight, d_normed, tokens, input_gain,
    d_resid, ffn_gains, query_gain_grad, grads, input_grad, gains,
):
    head_dim = key_pre.shape[1]
    width = tokens.shape[1]
    total = d_own[...] + d_near[...].astype(f32) + d_far[...].astype(f32)
    d_key = total[:, :head_dim].astype(bf16).astype(f32)
    d_value = total[:, head_dim:].astype(bf16)
    pre = key_pre[...]
    back, gain_part = rms_back(pre, rms_inverse(pre), key_gain[...], turn_back(d_key, cosine[...], sine[...]))
    back = back.astype(bf16)
    grads[:, :head_dim] = product(turned[...], back).astype(bf16)
    grads[:, head_dim:] = product(turned[...], d_value).astype(bf16)
    d_in = d_normed[...] + transposed_right(back, key_weight[...]) + transposed_right(d_value, value_weight[...])
    value = tokens[...].astype(f32)
    back, gain_in = rms_back(value, rms_inverse(value), input_gain[...], d_in)
    input_grad[...] = (d_resid[...] + back).astype(bf16)
    parts = [gain_in, query_gain_grad[...], gain_part] + [ffn_gains[row : row + 1, :] for row in (2, 1, 0)]
    full = jnp.concatenate(parts, axis=1)
    half = full.shape[1] // 2
    gains[0:1, :] = full[:, :half]
    gains[1:2, :] = full[:, half:]


def key_back(
    d_own, d_near, d_far, key_pre, cosine, sine, key_gain, turned, key_weight, value_weight, d_normed, tokens, input_gain,
    d_resid, ffn_gains, query_gain_grad,
):
    span, width = tokens.shape
    head_dim = key_pre.shape[1]
    vmem = pl.BlockSpec(memory_space=pltpu.VMEM)
    shape = jax.ShapeDtypeStruct
    return pl.pallas_call(
        key_back_kernel,
        out_shape=(
            shape((turned.shape[0], 2 * head_dim), bf16),
            shape((span, width), bf16),
            shape((2, 2 * width + head_dim), f32),
        ),
        in_specs=[vmem] * 16,
        out_specs=(vmem,) * 3,
        compiler_params=pltpu.CompilerParams(vmem_limit_bytes=48 * 1024 * 1024),
        cost_estimate=pl.CostEstimate(flops=10**9, bytes_accessed=6 * 2**20, transcendentals=0),
        name="key_back",
    )(
        d_own, d_near, d_far, key_pre, cosine, sine, key_gain[None], turned, key_weight, value_weight, d_normed, tokens,
        input_gain[None], d_resid, ffn_gains, query_gain_grad,
    )


def body(
    tokens,
    starts,
    query_weight,
    key_weight,
    value_weight,
    output_weight,
    gate_weight,
    up_weight,
    down_weight,
    input_gain,
    query_gain,
    key_gain,
    attn_gain,
    ffn_gain,
    ffn_out_gain,
    cotangent,
):
    span, width = tokens.shape
    head_dim = key_weight.shape[1]
    heads = query_weight.shape[1] // head_dim
    hq = heads * head_dim
    ff = gate_weight.shape[1]
    devices = lax.axis_size(ALL)
    hops = max(1, WINDOW // span)
    extent = hops * span + span
    scale = 1.0 / math.sqrt(head_dim)
    core = lax.axis_index("c")
    rows = query_weight.shape[0]
    columns = jnp.concatenate([gate_weight, up_weight], axis=1)
    columns = jnp.pad(columns, ((0, 8 - rows), (0, 0)))
    packed = jnp.concatenate([columns, output_weight, down_weight[:8], down_weight[8:]], axis=1)
    gathered = lax.all_gather(packed, ALL, axis=0, tiled=True)
    qkv = jnp.concatenate([query_weight, key_weight, value_weight], axis=1)
    qkv = lax.all_gather(jnp.pad(qkv, ((0, 8 - rows), (0, 0))), ("z", "c"), axis=0, tiled=False)
    qkv = qkv[:, :rows].reshape(8 * rows, -1)
    qkv = jnp.concatenate(
        [
            lax.dynamic_slice_in_dim(part, core * (part.shape[1] // 2), part.shape[1] // 2, 1)
            for part in (qkv[:, :hq], qkv[:, hq : hq + head_dim], qkv[:, hq + head_dim :])
        ],
        axis=1,
    )
    qkv = spread(jnp.broadcast_to(qkv, (16,) + qkv.shape), ("y", "x")).reshape(16 * 8 * rows, -1)
    other = swap_core(qkv)
    left = jnp.where(core == 0, qkv, other)
    right = jnp.where(core == 0, other, qkv)
    half, small = hq // 2, head_dim // 2
    full_query = jnp.concatenate([left[:, :half], right[:, :half]], axis=1)
    full_key = jnp.concatenate([left[:, half : half + small], right[:, half : half + small]], axis=1)
    full_value = jnp.concatenate([left[:, half + small :], right[:, half + small :]], axis=1)
    full_query, full_key, full_value = lax.optimization_barrier((full_query, full_key, full_value))

    place = jnp.arange(devices * 8, dtype=jnp.int32)
    pad_source = jnp.where(place % 8 < rows, place // 8 * rows + place % 8, -1)
    place = jnp.arange(width, dtype=jnp.int32)
    r, yx, c, z = place % rows, place // rows % 16, place // (rows * 16) % 2, place // (rows * 32)
    wide_source = ((yx * 4 + z) * 2 + c) * rows + r
    place = jnp.arange(2 * 16 * 24, dtype=jnp.int32)
    zr, x, y, c = place % 24, place // 24 % 4, place // (24 * 4) % 4, place // (24 * 16)
    c = jnp.where(core == 0, c, 1 - c)
    last_source = jnp.where(zr < 4 * rows, (((y * 4 + x) * 4 + zr // rows) * 2 + c) * rows + zr % rows, -1)

    group = lax.axis_index(ALL)
    group_ids = jnp.arange(starts.shape[0], dtype=jnp.int32)
    first_group = jnp.max(jnp.where((group_ids <= group) & (starts == 1), group_ids, 0))
    seq_first = first_group * span
    query_global = group * span + jnp.arange(span, dtype=jnp.int32)
    position = query_global - seq_first
    x_float = tokens.astype(jnp.float32)
    normed_in = rms_scale(x_float, input_gain).astype(bf16)
    query_pre = product(normed_in, full_query).reshape(span, heads, head_dim)
    key_pre = product(normed_in, full_key).reshape(span, 1, head_dim)
    value_bf = product(normed_in, full_value).astype(bf16)
    cosine, sine = rope_tables(position, head_dim)
    prepare = partial(head_prep, cosine=cosine, sine=sine)
    query_bf = prepare(query_pre, query_gain).astype(bf16)
    key_bf = prepare(key_pre, key_gain).astype(bf16).reshape(span, head_dim)
    pair = jnp.concatenate([key_bf, value_bf], axis=1)
    received = [shifted(pair, step) for step in range(hops, 0, -1)]
    both_all = jnp.concatenate(received + [pair], axis=0)
    keys_all = both_all[:, :head_dim]
    values_all = both_all[:, head_dim:]
    key_global = group * span - hops * span + jnp.arange(extent, dtype=jnp.int32)
    offset = query_global[:, None] - key_global[None, :]
    valid = (offset >= 0) & (offset < WINDOW) & (key_global[None, :] >= seq_first)
    query_flat = query_bf.reshape(span * heads, head_dim)
    scores = (transposed_right(query_flat, keys_all) * scale).reshape(span, heads, extent)
    scores = jnp.where(valid[:, None, :], scores, -1e30)
    peak = jnp.max(scores, axis=-1, keepdims=True)
    log_total = peak + jnp.log(jnp.sum(jnp.exp(scores - peak), axis=-1, keepdims=True))
    probs = jnp.exp(scores - log_total).reshape(span * heads, extent)
    probs_bf = probs.astype(bf16)
    attended_bf = product(probs_bf, values_all).reshape(span, heads * head_dim).astype(bf16)
    output, low_own, low_other, grads_wide, d_resid, d_attended_bf, ffn_gains = ffn(
        core.astype(jnp.int32).reshape(1), attended_bf, tokens, cotangent, gathered, attn_gain, ffn_gain, ffn_out_gain, pad_source, wide_source
    )
    wide = lax.psum_scatter(grads_wide, ("z", "c"), scatter_dimension=0, tiled=True)
    low_other = swap_core(low_other)
    bound = (seq_first - (group * span - hops * span)).reshape(1)
    cosine, sine = cosine[:, 0], sine[:, 0]
    d_own, d_near, d_far, d_query_pre_bf, grad_query_gain = attention_back(
        bound, query_bf.reshape(span, hq), both_all, d_attended_bf, query_pre.reshape(span, hq), cosine, sine, query_gain
    )
    d_near = shifted(d_near, -1)
    d_far = shifted(d_far, -2)
    part_low = (low_own.astype(f32) + low_other.astype(f32)).astype(bf16)
    d_query_pre_bf, part_low = lax.optimization_barrier((d_query_pre_bf, part_low))
    near_low = spread(part_low.reshape(16, 4 * 24, width), ("y", "x"))
    half_rows = last_source.shape[0] // 2
    grads_query, d_normed, turned = query_back(d_query_pre_bf, normed_in, last_source, full_query)
    other_query = swap_core(grads_query[half_rows:])
    grads_both, input_grad, gains = key_back(
        d_own, d_near, d_far, key_pre.reshape(span, head_dim), cosine, sine, key_gain, turned, full_key, full_value,
        d_normed, tokens, input_gain, d_resid, ffn_gains, grad_query_gain,
    )
    other_both = swap_core(grads_both[half_rows:])
    part_qkv = jnp.concatenate(
        [
            (grads_query[:half_rows].astype(f32) + other_query.astype(f32)).astype(bf16),
            (grads_both[:half_rows].astype(f32) + other_both.astype(f32)).astype(bf16),
        ],
        axis=1,
    ).reshape(16, 24, -1)

    gains = gains + swap_core(gains)
    carried = jnp.concatenate(high_low(gains), axis=0)
    part_qkv = jnp.concatenate(
        [part_qkv[:, : 4 * rows], jnp.broadcast_to(carried, (16,) + carried.shape)], axis=1
    )
    part_qkv, near_low, wide = lax.optimization_barrier((part_qkv, near_low, wide))
    near_qkv = spread(part_qkv, ("y", "x"))
    low = jnp.sum(near_low.astype(f32), axis=0)
    wide = jnp.pad(wide.reshape(4, 4 * rows, 2 * ff), ((0, 0), (0, 24 - 4 * rows), (0, 0)))
    wide = ring_sum(wide, "y")[: 4 * rows].astype(bf16).reshape(4, rows, 2 * ff)
    near_qkv, wide = lax.optimization_barrier((near_qkv, wide))
    wide = jnp.sum(spread(jnp.pad(wide, ((0, 0), (0, 8 - rows), (0, 0))), "x").astype(f32), axis=0)
    near_qkv = jnp.sum(near_qkv.astype(f32), axis=0)
    gains = (near_qkv[4 * rows : 4 * rows + 2] + near_qkv[4 * rows + 2 :]).reshape(4, -1)
    carried = jnp.concatenate(high_low(gains), axis=0)
    low = low.astype(bf16).reshape(4, 3, 8, width)
    low_columns = jnp.pad(near_qkv[: 4 * rows].astype(bf16).reshape(4, rows, -1), ((0, 0), (0, 8 - rows), (0, 0)))
    last = jnp.concatenate(
        [low_columns, low[:, 0], low[:, 1], low[:, 2], jnp.broadcast_to(carried, (4,) + carried.shape)],
        axis=2,
    )
    last = ring_sum(last, "z")
    sum_gate = wide[:rows, :ff]
    sum_up = wide[:rows, ff:]
    begin = hq + 2 * head_dim
    sum_qkv = last[:rows, :begin]
    sum_down = jnp.concatenate([last[:, begin : begin + width], last[:, begin + width : begin + 2 * width]], axis=0)
    sum_output = last[:, begin + 2 * width : begin + 3 * width]
    gains = last[:, begin + 3 * width :]
    gains = (gains[:4] + gains[4:]).reshape(-1)
    outs, begin = [], 0
    for size in (width, head_dim, head_dim, width, width, width):
        outs.append(gains[begin : begin + size])
        begin += size
    return (
        output,
        input_grad,
        sum_qkv[:, :hq],
        sum_qkv[:, hq : hq + head_dim],
        sum_qkv[:, hq + head_dim :],
        sum_output,
        sum_gate,
        sum_up,
        sum_down,
        *outs,
    )


def solution(mesh):
    inner = Mesh(mesh.devices.reshape(4, 4, 4, 2), ALL)
    split = P(ALL, None)
    return jax.shard_map(
        body,
        mesh=inner,
        in_specs=(split, P()) + (split,) * 7 + (P(),) * 6 + (split,),
        out_specs=(split,) * 9 + (P(),) * 6,
        check_vma=False,
    )
```

```python
from functools import partial
import math

import jax
import jax.numpy as jnp
from jax import lax
from jax.experimental import pallas as pl
from jax.experimental.pallas import tpu as pltpu
from jax.sharding import Mesh, PartitionSpec as P

WINDOW = 512
ALL = ("y", "x", "z", "c")

norm_epsilon = 1e-06
rope_base = 10000.0
GELU_A = math.sqrt(2.0 / math.pi)
GELU_B = 0.044715
bf16 = jnp.bfloat16
f32 = jnp.float32


def shifted(value, steps):
    count = lax.axis_size(ALL)
    leading, last = (max(0, -steps), min(count, count - steps))
    return lax.ppermute(value, ALL, [(source, source + steps) for source in range(leading, last)])


def rms_scale(values, gain):
    mean_square = jnp.mean(values * values, axis=-1, keepdims=True)
    return values * lax.rsqrt(mean_square + norm_epsilon) * gain


def rope_tables(position, head_dim):
    half = head_dim // 2
    exponent = jnp.arange(half, dtype=jnp.float32) * (2.0 / head_dim)
    inverse = jnp.power(jnp.float32(rope_base), -exponent)
    angles = position.astype(jnp.float32)[:, None] * inverse[None, :]
    return (jnp.cos(angles)[:, None, :], jnp.sin(angles)[:, None, :])


def head_prep(pre, gain, cosine, sine):
    normed = rms_scale(pre, gain)
    half = normed.shape[-1] // 2
    first = normed[..., :half]
    second = normed[..., half:]
    return jnp.concatenate(
        [first * cosine - second * sine, second * cosine + first * sine], axis=-1
    )


def gated(gate, upward):
    return jax.nn.gelu(gate, approximate=True) * upward


def product(left, right):
    return jnp.dot(left, right, preferred_element_type=jnp.float32)


def transposed_left(left, right):
    return lax.dot_general(
        left, right, (((0,), (0,)), ((), ())), preferred_element_type=jnp.float32
    )


def transposed_right(left, right):
    return lax.dot_general(
        left, right, (((1,), (1,)), ((), ())), preferred_element_type=jnp.float32
    )


def swap_core(value):
    return lax.ppermute(value, "c", [(0, 1), (1, 0)])


def halves(value, axis):
    core = lax.axis_index("c")
    mine = lax.dynamic_index_in_dim(value, core, axis, keepdims=False)
    theirs = lax.dynamic_index_in_dim(value, 1 - core, axis, keepdims=False)
    return mine, theirs


def core_sum(value, axis):
    mine, theirs = halves(value.astype(bf16), axis)
    return (mine.astype(f32) + swap_core(theirs).astype(f32)).astype(bf16)


def chosen(rows, source):
    return (jnp.arange(rows, dtype=jnp.int32)[:, None] == source[None, :]).astype(bf16)


def spread(value, axes):
    return lax.all_to_all(value, axes, split_axis=0, concat_axis=0, tiled=True)


def ring_sum(blocks, axis):
    place = lax.axis_index(axis)
    total = lax.dynamic_index_in_dim(blocks, place, 0, keepdims=False).astype(f32)
    for step in (1, 3, 2):
        block = lax.dynamic_index_in_dim(blocks, lax.rem(place + step, 4), 0, keepdims=False)
        total = total + lax.ppermute(block, axis, [(i, (i + step) % 4) for i in range(4)]).astype(f32)
    return total


def high_low(value):
    high = value.astype(bf16)
    low = (value - high.astype(f32)).astype(bf16)
    return high, low


def rms_inverse(values):
    return lax.rsqrt(jnp.mean(values * values, axis=-1, keepdims=True) + norm_epsilon)


def rms_back(values, inverse, gain, grad):
    scaled = grad * gain
    kept = values * inverse
    back = inverse * (scaled - kept * jnp.mean(scaled * kept, axis=-1, keepdims=True))
    return back, jnp.sum(grad * kept, axis=0, keepdims=True)


def one_hot(source, count):
    return (lax.broadcasted_iota(jnp.int32, (count, source.shape[1]), 0) == source).astype(f32).astype(bf16)


CHUNK = 1024


def ffn_kernel(
    core, attended, tokens, cotangent, gathered, attn_gain, ffn_gain, out_gain, pad_source, last_source,
    output, grad_own, grad_other, grad_wide, d_resid, d_attended, gains,
    grad_low, wide, low, first, second, mixed, normed_pad, normed_turned, projected, resid, pad_rows, d_down, down, d_pad, down_rows, sems,
):
    span, width = tokens.shape
    ff = mixed.shape[1]
    steps = ff // CHUNK
    copies = [pltpu.make_async_copy(gathered.at[:, 2 * ff :], low, sems.at[0])]
    for step in range(2 * steps):
        part = pl.ds((step // 2) * CHUNK + (step % 2) * ff, CHUNK)
        copies.append(pltpu.make_async_copy(gathered.at[:, part], wide.at[:, part], sems.at[1 + step]))
    for copy in copies:
        copy.start()
    pad_rows[...] = one_hot(pad_source[...], width)
    copies[0].wait()
    projected[...] = product(attended[...], low[:, :width])
    value = projected[...]
    resid[...] = tokens[...].astype(f32) + value * rms_inverse(value) * attn_gain[...]
    value = resid[...]
    normed = (value * rms_inverse(value) * ffn_gain[...]).astype(bf16)
    normed_pad[...] = product(normed, pad_rows[...]).astype(bf16)
    normed_turned[...] = product(normed, one_hot(last_source[...], width)).astype(bf16).T
    down[...] = jnp.zeros_like(down)

    for step in range(steps):
        block = pl.ds(step * (CHUNK // 2), CHUNK // 2)
        parts = [low[block, begin : begin + width].astype(f32).reshape(CHUNK // 16, 8, width) for begin in (width, 2 * width)]
        down_rows[step * CHUNK : (step + 1) * CHUNK, :] = (
            jnp.concatenate(parts, axis=1).reshape(CHUNK, width).astype(bf16)
        )

    for step in range(steps):
        here = pl.ds(step * CHUNK, CHUNK)
        there = pl.ds(ff + step * CHUNK, CHUNK)
        copies[1 + 2 * step].wait()
        copies[2 + 2 * step].wait()
        gate = product(normed_pad[...], wide[:, here])
        upward = product(normed_pad[...], wide[:, there])
        square = gate * gate
        bend = jnp.tanh(gate * (GELU_A + GELU_A * GELU_B * square))
        half = 0.5 + 0.5 * bend
        curve = gate * half
        slope = half + 0.5 * gate * (1.0 - bend * bend) * (GELU_A + 3.0 * GELU_A * GELU_B * square)
        first[:, here] = curve
        second[:, here] = slope * upward
        mixed[:, here] = (curve * upward).astype(bf16)
        down[...] += product(mixed[:, here], down_rows[here, :])

    value = down[...]
    inverse = rms_inverse(value)
    output[...] = (resid[...] + value * inverse * out_gain[...]).astype(bf16)
    back, gains[0:1, :] = rms_back(value, inverse, out_gain[...], cotangent[...].astype(f32))
    d_down[...] = back.astype(bf16)
    d_pad[...] = jnp.zeros_like(d_pad)
    for step in range(steps):
        here = pl.ds(step * CHUNK, CHUNK)
        there = pl.ds(ff + step * CHUNK, CHUNK)
        grad = transposed_left(mixed[:, here], d_down[...]).astype(bf16).reshape(CHUNK // 128, 4, 2, 16, width)
        blocks = pl.ds(step * (CHUNK // 128), CHUNK // 128)
        grad_low[0, blocks, :, :16] = grad[:, :, 0]
        grad_low[1, blocks, :, :16] = grad[:, :, 1]
        d_mixed = transposed_right(d_down[...], down_rows[here, :])
        d_gate = (d_mixed * second[:, here]).astype(bf16)
        d_upward = (d_mixed * first[:, here]).astype(bf16)
        grad_wide[:, here] = product(normed_turned[...], d_gate).astype(bf16)
        grad_wide[:, there] = product(normed_turned[...], d_upward).astype(bf16)
        d_pad[...] += transposed_right(d_gate, wide[:, here]) + transposed_right(d_upward, wide[:, there])
    out_copies = []
    for half, grad in enumerate((grad_own, grad_other)):
        source = grad_low.at[core[0] if half == 0 else 1 - core[0]]
        out_copies.append(pltpu.make_async_copy(source.at[:, :, :16], grad.at[:, :, :16], sems.at[half]))
        out_copies.append(pltpu.make_async_copy(source.at[:, :, 16:], grad.at[:, :, 16:], sems.at[2 + half]))
    out_copies[0].start()
    out_copies[2].start()
    high, lower = high_low(d_pad[...])
    d_normed = transposed_right(high, pad_rows[...]) + transposed_right(lower, pad_rows[...])
    value = resid[...]
    back, gains[1:2, :] = rms_back(value, rms_inverse(value), ffn_gain[...], d_normed)
    back = cotangent[...].astype(f32) + back
    d_resid[...] = back
    value = projected[...]
    back, gains[2:3, :] = rms_back(value, rms_inverse(value), attn_gain[...], back)
    back = back.astype(bf16)
    grad = transposed_left(attended[...], back).reshape(16, 4, 2, 8, width)
    grad_low[0, :, :, 16:] = grad[:, :, 0].astype(bf16)
    grad_low[1, :, :, 16:] = grad[:, :, 1].astype(bf16)
    out_copies[1].start()
    out_copies[3].start()
    d_attended[...] = transposed_right(back, low[:, :width]).astype(bf16)
    for copy in out_copies:
        copy.wait()


def ffn(core, attended, tokens, cotangent, gathered, attn_gain, ffn_gain, out_gain, pad_source, last_source):
    span, width = tokens.shape
    hq = attended.shape[1]
    ff = (gathered.shape[1] - 3 * width) // 2
    padded, spaced = gathered.shape[0], last_source.shape[0]
    vmem = pl.BlockSpec(memory_space=pltpu.VMEM)
    shape = jax.ShapeDtypeStruct
    return pl.pallas_call(
        ffn_kernel,
        out_shape=(
            shape((span, width), bf16),
            shape((16, 4, 24, width), bf16),
            shape((16, 4, 24, width), bf16),
            shape((spaced, 2 * ff), bf16),
            shape((span, width), f32),
            shape((span, hq), bf16),
            shape((3, width), f32),
        ),
        in_specs=[pl.BlockSpec(memory_space=pltpu.SMEM)] + [vmem] * 3 + [pl.BlockSpec(memory_space=pl.ANY)] + [vmem] * 5,
        out_specs=(vmem, pl.BlockSpec(memory_space=pl.ANY), pl.BlockSpec(memory_space=pl.ANY)) + (vmem,) * 4,
        scratch_shapes=[
            pltpu.VMEM((2, 16, 4, 24, width), bf16),
            pltpu.VMEM((padded, 2 * ff), bf16),
            pltpu.VMEM((padded, 3 * width), bf16),
            pltpu.VMEM((span, ff), f32),
            pltpu.VMEM((span, ff), f32),
            pltpu.VMEM((span, ff), bf16),
            pltpu.VMEM((span, padded), bf16),
            pltpu.VMEM((spaced, span), bf16),
            pltpu.VMEM((span, width), f32),
            pltpu.VMEM((span, width), f32),
            pltpu.VMEM((width, padded), bf16),
            pltpu.VMEM((span, width), bf16),
            pltpu.VMEM((span, width), f32),
            pltpu.VMEM((span, padded), f32),
            pltpu.VMEM((ff, width), bf16),
            pltpu.SemaphoreType.DMA((1 + 2 * (ff // CHUNK),)),
        ],
        compiler_params=pltpu.CompilerParams(vmem_limit_bytes=56 * 1024 * 1024),
        cost_estimate=pl.CostEstimate(flops=9 * 10**9, bytes_accessed=24 * 2**20, transcendentals=span * ff),
        name="ffn",
    )(
        core, attended, tokens, cotangent, gathered, attn_gain[None], ffn_gain[None], out_gain[None],
        pad_source[None], last_source[None],
    )


def turn_back(grad, cosine, sine):
    half = grad.shape[1] // 2
    first, second = grad[:, :half], grad[:, half:]
    return jnp.concatenate([first * cosine + second * sine, second * cosine - first * sine], axis=1)


def attention_back_kernel(
    bound, queries, both, d_attended, query_pre, cosine, sine, query_gain,
    d_own, d_near, d_far, d_query_pre, grad_gain, d_both,
):
    span, hq = queries.shape
    extent = both.shape[0]
    head_dim = both.shape[1] // 2
    scale = 1.0 / math.sqrt(head_dim)
    offset = (
        lax.broadcasted_iota(jnp.int32, (span, extent), 0)
        - lax.broadcasted_iota(jnp.int32, (span, extent), 1)
        + (extent - span)
    )
    place = lax.broadcasted_iota(jnp.int32, (span, extent), 1)
    valid = (offset >= 0) & (offset < WINDOW) & (place >= bound[0])
    keys, values = both[:, :head_dim], both[:, head_dim:]
    gain_sum = jnp.zeros((1, head_dim), f32)
    for head in range(hq // head_dim):
        here = pl.ds(head * head_dim, head_dim)
        query, d_att = queries[:, here], d_attended[:, here]
        scores = jnp.where(valid, transposed_right(query, keys) * scale, -1e30)
        weights = jnp.exp(scores - jnp.max(scores, axis=-1, keepdims=True))
        probs = weights * (1.0 / jnp.sum(weights, axis=-1, keepdims=True))
        d_probs = transposed_right(d_att, values)
        balance = jnp.sum(d_probs * probs, axis=-1, keepdims=True)
        d_scores = (probs * (d_probs - balance)).astype(bf16)
        d_query = (product(d_scores, keys) * scale).astype(bf16).astype(f32)
        d_key = transposed_left(d_scores, query) * scale
        d_value = transposed_left(probs.astype(bf16), d_att)
        if head == 0:
            d_both[:, :head_dim] = d_key
            d_both[:, head_dim:] = d_value
        else:
            d_both[:, :head_dim] += d_key
            d_both[:, head_dim:] += d_value
        pre = query_pre[:, here]
        back, gain_part = rms_back(pre, rms_inverse(pre), query_gain[...], turn_back(d_query, cosine[...], sine[...]))
        gain_sum += gain_part
        d_query_pre[:, here] = back.astype(bf16)
    grad_gain[...] = gain_sum
    d_far[...] = d_both[:span, :].astype(bf16)
    d_near[...] = d_both[span : 2 * span, :].astype(bf16)
    d_own[...] = d_both[2 * span :, :]


def attention_back(bound, queries, both, d_attended, query_pre, cosine, sine, query_gain):
    span, hq = queries.shape
    extent, pair = both.shape
    vmem = pl.BlockSpec(memory_space=pltpu.VMEM)
    shape = jax.ShapeDtypeStruct
    return pl.pallas_call(
        attention_back_kernel,
        out_shape=(
            shape((span, pair), f32),
            shape((span, pair), bf16),
            shape((span, pair), bf16),
            shape((span, hq), bf16),
            shape((1, pair // 2), f32),
        ),
        in_specs=[pl.BlockSpec(memory_space=pltpu.SMEM)] + [vmem] * 7,
        out_specs=(vmem,) * 5,
        scratch_shapes=[pltpu.VMEM((extent, pair), f32)],
        compiler_params=pltpu.CompilerParams(vmem_limit_bytes=48 * 1024 * 1024),
        cost_estimate=pl.CostEstimate(flops=12 * span * extent * hq, bytes_accessed=6 * 2**20, transcendentals=4 * span * extent),
        name="attention_back",
    )(bound, queries, both, d_attended, query_pre, cosine, sine, query_gain[None])


def query_back_kernel(d_query_pre, normed, source, weight, grads, d_normed, turned):
    turned[...] = product(normed[...], one_hot(source[...], normed.shape[1])).astype(bf16).T
    grads[...] = product(turned[...], d_query_pre[...]).astype(bf16)
    d_normed[...] = transposed_right(d_query_pre[...], weight[...])


def query_back(d_query_pre, normed, source, weight):
    span, width = normed.shape
    vmem = pl.BlockSpec(memory_space=pltpu.VMEM)
    shape = jax.ShapeDtypeStruct
    return pl.pallas_call(
        query_back_kernel,
        out_shape=(
            shape((source.shape[0], d_query_pre.shape[1]), bf16),
            shape((span, width), f32),
            shape((source.shape[0], span), bf16),
        ),
        in_specs=[vmem] * 4,
        out_specs=(vmem,) * 3,
        compiler_params=pltpu.CompilerParams(vmem_limit_bytes=48 * 1024 * 1024),
        cost_estimate=pl.CostEstimate(flops=10**9, bytes_accessed=4 * 2**20, transcendentals=0),
        name="query_back",
    )(d_query_pre, normed, source[None], weight)


def key_back_kernel(
    d_own, d_near, d_far, key_pre, cosine, sine, key_gain, turned, key_weight, value_weight, d_normed, tokens, input_gain,
    d_resid, ffn_gains, query_gain_grad, grads, input_grad, gains,
):
    head_dim = key_pre.shape[1]
    width = tokens.shape[1]
    total = d_own[...] + d_near[...].astype(f32) + d_far[...].astype(f32)
    d_key = total[:, :head_dim].astype(bf16).astype(f32)
    d_value = total[:, head_dim:].astype(bf16)
    pre = key_pre[...]
    back, gain_part = rms_back(pre, rms_inverse(pre), key_gain[...], turn_back(d_key, cosine[...], sine[...]))
    back = back.astype(bf16)
    grads[:, :head_dim] = product(turned[...], back).astype(bf16)
    grads[:, head_dim:] = product(turned[...], d_value).astype(bf16)
    d_in = d_normed[...] + transposed_right(back, key_weight[...]) + transposed_right(d_value, value_weight[...])
    value = tokens[...].astype(f32)
    back, gain_in = rms_back(value, rms_inverse(value), input_gain[...], d_in)
    input_grad[...] = (d_resid[...] + back).astype(bf16)
    parts = [gain_in, query_gain_grad[...], gain_part] + [ffn_gains[row : row + 1, :] for row in (2, 1, 0)]
    full = jnp.concatenate(parts, axis=1)
    half = full.shape[1] // 2
    gains[0:1, :] = full[:, :half]
    gains[1:2, :] = full[:, half:]


def key_back(
    d_own, d_near, d_far, key_pre, cosine, sine, key_gain, turned, key_weight, value_weight, d_normed, tokens, input_gain,
    d_resid, ffn_gains, query_gain_grad,
):
    span, width = tokens.shape
    head_dim = key_pre.shape[1]
    vmem = pl.BlockSpec(memory_space=pltpu.VMEM)
    shape = jax.ShapeDtypeStruct
    return pl.pallas_call(
        key_back_kernel,
        out_shape=(
            shape((turned.shape[0], 2 * head_dim), bf16),
            shape((span, width), bf16),
            shape((2, 2 * width + head_dim), f32),
        ),
        in_specs=[vmem] * 16,
        out_specs=(vmem,) * 3,
        compiler_params=pltpu.CompilerParams(vmem_limit_bytes=48 * 1024 * 1024),
        cost_estimate=pl.CostEstimate(flops=10**9, bytes_accessed=6 * 2**20, transcendentals=0),
        name="key_back",
    )(
        d_own, d_near, d_far, key_pre, cosine, sine, key_gain[None], turned, key_weight, value_weight, d_normed, tokens,
        input_gain[None], d_resid, ffn_gains, query_gain_grad,
    )


def body(
    tokens,
    starts,
    query_weight,
    key_weight,
    value_weight,
    output_weight,
    gate_weight,
    up_weight,
    down_weight,
    input_gain,
    query_gain,
    key_gain,
    attn_gain,
    ffn_gain,
    ffn_out_gain,
    cotangent,
):
    span, width = tokens.shape
    head_dim = key_weight.shape[1]
    heads = query_weight.shape[1] // head_dim
    hq = heads * head_dim
    ff = gate_weight.shape[1]
    devices = lax.axis_size(ALL)
    hops = max(1, WINDOW // span)
    extent = hops * span + span
    scale = 1.0 / math.sqrt(head_dim)
    core = lax.axis_index("c")
    rows = query_weight.shape[0]
    columns = jnp.concatenate([gate_weight, up_weight], axis=1)
    columns = jnp.pad(columns, ((0, 8 - rows), (0, 0)))
    packed = jnp.concatenate([columns, output_weight, down_weight[:8], down_weight[8:]], axis=1)
    gathered = lax.all_gather(packed, ALL, axis=0, tiled=True)
    qkv = jnp.concatenate([query_weight, key_weight, value_weight], axis=1)
    qkv = lax.all_gather(jnp.pad(qkv, ((0, 8 - rows), (0, 0))), ("z", "c"), axis=0, tiled=False)
    qkv = qkv[:, :rows].reshape(8 * rows, -1)
    qkv = jnp.concatenate(
        [
            lax.dynamic_slice_in_dim(part, core * (part.shape[1] // 2), part.shape[1] // 2, 1)
            for part in (qkv[:, :hq], qkv[:, hq : hq + head_dim], qkv[:, hq + head_dim :])
        ],
        axis=1,
    )
    qkv = spread(jnp.broadcast_to(qkv, (16,) + qkv.shape), ("y", "x")).reshape(16 * 8 * rows, -1)
    other = swap_core(qkv)
    left = jnp.where(core == 0, qkv, other)
    right = jnp.where(core == 0, other, qkv)
    half, small = hq // 2, head_dim // 2
    full_query = jnp.concatenate([left[:, :half], right[:, :half]], axis=1)
    full_key = jnp.concatenate([left[:, half : half + small], right[:, half : half + small]], axis=1)
    full_value = jnp.concatenate([left[:, half + small :], right[:, half + small :]], axis=1)
    full_query, full_key, full_value = lax.optimization_barrier((full_query, full_key, full_value))

    place = jnp.arange(devices * 8, dtype=jnp.int32)
    pad_source = jnp.where(place % 8 < rows, place // 8 * rows + place % 8, -1)
    place = jnp.arange(width, dtype=jnp.int32)
    r, yx, c, z = place % rows, place // rows % 16, place // (rows * 16) % 2, place // (rows * 32)
    wide_source = ((yx * 4 + z) * 2 + c) * rows + r
    place = jnp.arange(2 * 16 * 24, dtype=jnp.int32)
    zr, x, y, c = place % 24, place // 24 % 4, place // (24 * 4) % 4, place // (24 * 16)
    c = jnp.where(core == 0, c, 1 - c)
    last_source = jnp.where(zr < 4 * rows, (((y * 4 + x) * 4 + zr // rows) * 2 + c) * rows + zr % rows, -1)

    group = lax.axis_index(ALL)
    group_ids = jnp.arange(starts.shape[0], dtype=jnp.int32)
    first_group = jnp.max(jnp.where((group_ids <= group) & (starts == 1), group_ids, 0))
    seq_first = first_group * span
    query_global = group * span + jnp.arange(span, dtype=jnp.int32)
    position = query_global - seq_first
    x_float = tokens.astype(jnp.float32)
    normed_in = rms_scale(x_float, input_gain).astype(bf16)
    query_pre = product(normed_in, full_query).reshape(span, heads, head_dim)
    key_pre = product(normed_in, full_key).reshape(span, 1, head_dim)
    value_bf = product(normed_in, full_value).astype(bf16)
    cosine, sine = rope_tables(position, head_dim)
    prepare = partial(head_prep, cosine=cosine, sine=sine)
    query_bf = prepare(query_pre, query_gain).astype(bf16)
    key_bf = prepare(key_pre, key_gain).astype(bf16).reshape(span, head_dim)
    pair = jnp.concatenate([key_bf, value_bf], axis=1)
    received = [shifted(pair, step) for step in range(hops, 0, -1)]
    both_all = jnp.concatenate(received + [pair], axis=0)
    keys_all = both_all[:, :head_dim]
    values_all = both_all[:, head_dim:]
    key_global = group * span - hops * span + jnp.arange(extent, dtype=jnp.int32)
    offset = query_global[:, None] - key_global[None, :]
    valid = (offset >= 0) & (offset < WINDOW) & (key_global[None, :] >= seq_first)
    query_flat = query_bf.reshape(span * heads, head_dim)
    scores = (transposed_right(query_flat, keys_all) * scale).reshape(span, heads, extent)
    scores = jnp.where(valid[:, None, :], scores, -1e30)
    peak = jnp.max(scores, axis=-1, keepdims=True)
    log_total = peak + jnp.log(jnp.sum(jnp.exp(scores - peak), axis=-1, keepdims=True))
    probs = jnp.exp(scores - log_total).reshape(span * heads, extent)
    probs_bf = probs.astype(bf16)
    attended_bf = product(probs_bf, values_all).reshape(span, heads * head_dim).astype(bf16)
    output, low_own, low_other, grads_wide, d_resid, d_attended_bf, ffn_gains = ffn(
        core.astype(jnp.int32).reshape(1), attended_bf, tokens, cotangent, gathered, attn_gain, ffn_gain, ffn_out_gain, pad_source, wide_source
    )
    wide = lax.psum_scatter(grads_wide, ("z", "c"), scatter_dimension=0, tiled=True)
    low_other = swap_core(low_other)
    bound = (seq_first - (group * span - hops * span)).reshape(1)
    cosine, sine = cosine[:, 0], sine[:, 0]
    d_own, d_near, d_far, d_query_pre_bf, grad_query_gain = attention_back(
        bound, query_bf.reshape(span, hq), both_all, d_attended_bf, query_pre.reshape(span, hq), cosine, sine, query_gain
    )
    d_near = shifted(d_near, -1)
    d_far = shifted(d_far, -2)
    part_low = (low_own.astype(f32) + low_other.astype(f32)).astype(bf16)
    d_query_pre_bf, part_low = lax.optimization_barrier((d_query_pre_bf, part_low))
    near_low = spread(part_low.reshape(16, 4 * 24, width), ("y", "x"))
    half_rows = last_source.shape[0] // 2
    grads_query, d_normed, turned = query_back(d_query_pre_bf, normed_in, last_source, full_query)
    other_query = swap_core(grads_query[half_rows:])
    grads_both, input_grad, gains = key_back(
        d_own, d_near, d_far, key_pre.reshape(span, head_dim), cosine, sine, key_gain, turned, full_key, full_value,
        d_normed, tokens, input_gain, d_resid, ffn_gains, grad_query_gain,
    )
    other_both = swap_core(grads_both[half_rows:])
    part_qkv = jnp.concatenate(
        [
            (grads_query[:half_rows].astype(f32) + other_query.astype(f32)).astype(bf16),
            (grads_both[:half_rows].astype(f32) + other_both.astype(f32)).astype(bf16),
        ],
        axis=1,
    ).reshape(16, 24, -1)

    gains = gains + swap_core(gains)
    carried = jnp.concatenate(high_low(gains), axis=0)
    part_qkv = jnp.concatenate(
        [part_qkv[:, : 4 * rows], jnp.broadcast_to(carried, (16,) + carried.shape)], axis=1
    )
    wide = jnp.pad(wide.reshape(4, 4 * rows, 2 * ff), ((0, 0), (0, 24 - 4 * rows), (0, 0)))
    part_qkv, near_low, wide = lax.optimization_barrier((part_qkv, near_low, wide))
    near_qkv = spread(part_qkv, ("y", "x"))
    low = jnp.sum(near_low.astype(f32), axis=0)
    wide = ring_sum(wide, "y")[: 4 * rows].astype(bf16).reshape(4, rows, 2 * ff)
    near_qkv, wide = lax.optimization_barrier((near_qkv, wide))
    wide = jnp.sum(spread(jnp.pad(wide, ((0, 0), (0, 8 - rows), (0, 0))), "x").astype(f32), axis=0)
    near_qkv = jnp.sum(near_qkv.astype(f32), axis=0)
    gains = (near_qkv[4 * rows : 4 * rows + 2] + near_qkv[4 * rows + 2 :]).reshape(4, -1)
    carried = jnp.concatenate(high_low(gains), axis=0)
    low = low.astype(bf16).reshape(4, 3, 8, width)
    low_columns = jnp.pad(near_qkv[: 4 * rows].astype(bf16).reshape(4, rows, -1), ((0, 0), (0, 8 - rows), (0, 0)))
    last = jnp.concatenate(
        [low_columns, low[:, 0], low[:, 1], low[:, 2], jnp.broadcast_to(carried, (4,) + carried.shape)],
        axis=2,
    )
    last = ring_sum(last, "z")
    sum_gate = wide[:rows, :ff]
    sum_up = wide[:rows, ff:]
    begin = hq + 2 * head_dim
    sum_qkv = last[:rows, :begin]
    sum_down = jnp.concatenate([last[:, begin : begin + width], last[:, begin + width : begin + 2 * width]], axis=0)
    sum_output = last[:, begin + 2 * width : begin + 3 * width]
    gains = last[:, begin + 3 * width :]
    gains = (gains[:4] + gains[4:]).reshape(-1)
    outs, begin = [], 0
    for size in (width, head_dim, head_dim, width, width, width):
        outs.append(gains[begin : begin + size])
        begin += size
    return (
        output,
        input_grad,
        sum_qkv[:, :hq],
        sum_qkv[:, hq : hq + head_dim],
        sum_qkv[:, hq + head_dim :],
        sum_output,
        sum_gate,
        sum_up,
        sum_down,
        *outs,
    )


def solution(mesh):
    inner = Mesh(mesh.devices.reshape(4, 4, 4, 2), ALL)
    split = P(ALL, None)
    return jax.shard_map(
        body,
        mesh=inner,
        in_specs=(split, P()) + (split,) * 7 + (P(),) * 6 + (split,),
        out_specs=(split,) * 9 + (P(),) * 6,
        check_vma=False,
    )
```
